128 devices in a mesh: dp: 4 (over y), seq: 2 (over core), expert: 16 (over z, x).
Axes of the slice: x: 4, y: 4, z: 4, core: 2. Of those that a mesh axis runs over, the one named last changes fastest.
Arguments:
- hidden_in: bfloat16 [16384, 1152], P(('dp', 'seq', 'expert')), may hold values from -6 to 6
- grad_out: bfloat16 [16384, 1152], P(('dp', 'seq', 'expert')), may hold values from -1.5 to 1.5
- combine: float32 [16384, 2], P(('dp', 'seq', 'expert')), may hold values from 0.1 to 1
- routes: int32 [16384, 2], P(('dp', 'seq', 'expert')), may hold values from 0 to 15, all different within a row; in each aligned block of 128 rows (0 to 127, 128 to 255, ...) at most 20 rows name the same one
- w_in: bfloat16 [16, 1152, 4608], P('expert', None, ('dp', 'seq')), may hold values from -0.1875 to 0.1875
- w_out: bfloat16 [16, 4608, 1152], P('expert', ('dp', 'seq')), may hold values from -0.09375 to 0.09375
Outputs:
- grad_x: bfloat16 [16384, 1152], P(('dp', 'seq', 'expert'))
- grad_combine: float32 [16384, 2], P(('dp', 'seq', 'expert'))
- grad_w_in: bfloat16 [16, 1152, 4608], P('expert', None, ('dp', 'seq'))
- grad_w_out: bfloat16 [16, 4608, 1152], P('expert', ('dp', 'seq'))
The draws below stay inside these ranges and needn't reach their ends.
Inputs may be any that keep to these rules, and one draw needn't show every extreme that they name: `routes`: each token names 2 different experts. Within the 128 tokens of one device (aligned blocks of rows) no expert is named by more than 20 tokens, and in every draw some expert is named by exactly 20 tokens of some block.
All inputs are finite; a program needn't handle non-finite values.
Results may differ from the reference program's by a relative error of at most 0.023.
Values may be sent and summed in bfloat16 or wider, within the bound.
No kernel may reach another device: no remote copies, remote signals or barrier semaphores. Data moves between devices by JAX's collectives and lax.ppermute only.
A program may use at most 128 MiB of HBM per device.

```python
import math
import jax
import jax.numpy as jnp
import numpy as np
from jax import lax

D = 1152
FF = 4608
TOP = 2
TOK_DEV = 128
EXPERTS = 16
CAP = 20
TOKENS = 16384


def level_of(key, extent, split, smallest, high):
    level, own = 1.0, jax.random.fold_in(key, 6)
    for axis_at, blocks in split:
        heights = jnp.exp(jax.random.uniform(jax.random.fold_in(own, axis_at), (blocks,), jnp.float32, smallest / len(split), high / len(split)))
        level = level * jnp.repeat(heights, extent[axis_at] // blocks).reshape([-1 if axis == axis_at else 1 for axis in range(len(extent))])
    return level


def assign_block(rng, own, number, rows, amount, top, reach, skew):
    order = jax.random.permutation(rng, amount)
    heavy_load, ordinary = load_shares(amount, rows * top, reach, skew, True), load_shares(amount, rows * top, reach, skew, False)
    places = jnp.arange(amount)

    def named(sizes, offset_by):
        used = int((sizes > 0).sum())
        fixed = max(1, used // 4)
        moved = fixed + (places - fixed + offset_by * (used - fixed)) % max(1, amount - fixed)
        return jnp.zeros((amount,), jnp.int32).at[order[jnp.where(places < fixed, places, moved)]].set(jnp.asarray(sizes, jnp.int32))

    sizes = jnp.where(number % 4 == 0, named(heavy_load, number // 4), named(ordinary, number - number // 4 - 1))
    mixed = jax.random.permutation(jax.random.fold_in(own, 3), amount)
    giver, receiver = mixed[0:amount // 2 * 2:2], mixed[1:amount // 2 * 2:2]
    room = jnp.minimum(sizes[giver] - 1, reach - sizes[receiver]) // 2
    room = jnp.where((giver == order[0]) | (receiver == order[0]) | (sizes[receiver] == 0), 0, jnp.maximum(room, 0))
    moved = jax.random.randint(jax.random.fold_in(own, 4), (amount // 2,), 0, 1 << 20) % (room + 1)
    sizes = sizes.at[giver].add(-moved).at[receiver].add(moved)
    members = jnp.searchsorted(jnp.cumsum(sizes), jnp.arange(rows * top), side="right").astype(jnp.int32)
    grid = members.reshape(top, rows).T
    grid = grid[jax.random.permutation(jax.random.fold_in(own, 1), rows)]
    offset_by = jax.random.randint(jax.random.fold_in(own, 2), (rows, 1), 0, top)
    return jnp.take_along_axis(grid, (jnp.arange(top)[None, :] + offset_by) % top, axis=1)


def load_shares(number_of, total, bound, slope, full):
    loads = [(1 << 20) // math.isqrt(rank ** slope) + 1 for rank in range(1, number_of + 1)]
    largest = bound if full else min(bound, max(-(-total // number_of), total * loads[0] // sum(loads)))
    least = 1 if total - largest >= number_of - 1 else 0
    counts, spare = [largest] + [least] * (number_of - 1), total - largest - least * (number_of - 1)
    while spare > 0:
        free = [i for i in range(1, number_of) if counts[i] < largest] or [i for i in range(1, number_of) if counts[i] < bound]
        pool, budget = sum([loads[i] for i in free]), spare
        for i in free:
            more = min(bound - counts[i], max(1, budget * loads[i] // pool), spare)
            counts[i] = counts[i] + more
            spare = spare - more
    return np.array(counts)


def noise(own_key, extent, scale, most, split=(), kind=jnp.bfloat16):
    entries = scale * jax.random.normal(own_key, extent, jnp.float32)
    if split:
        entries = entries * level_of(own_key, extent, split, -0.22, 0.18)
    return jnp.clip(entries, -most, most).astype(kind)


def setup_inputs(seed: int = 0) -> dict:
    seeds = jax.random.split(jax.random.key(seed), 7)
    hidden_in = noise(seeds[0], (TOKENS, D), 1.0, 6.0, ((0, 128),))
    grad_out = noise(seeds[1], (TOKENS, D), 0.25, 1.5, ((0, 128),))
    combine = jnp.clip(0.1 + 0.9 * jax.random.uniform(seeds[2], (TOKENS, TOP), jnp.float32) ** level_of(seeds[2], (TOKENS, TOP), ((0, 128),), -0.2, 0.2), 0.1, 1.0)
    routes_keys = jax.random.split(jax.random.fold_in(seeds[3], 1), TOKENS // TOK_DEV)
    routes_turns = jax.random.permutation(jax.random.fold_in(seeds[3], 3), TOKENS // TOK_DEV)
    routes = jax.vmap(lambda own, number: assign_block(jax.random.fold_in(seeds[3], 2), own, number, TOK_DEV, EXPERTS, TOP, CAP, 2))(routes_keys, routes_turns).reshape((TOKENS, TOP))
    w_in = noise(seeds[4], (EXPERTS, D, FF), D ** -0.5, 0.1875, ((0, 16), (2, 8)))
    w_out = noise(seeds[5], (EXPERTS, FF, D), FF ** -0.5, 0.09375, ((0, 16), (1, 8)))
    return dict(hidden_in=hidden_in, grad_out=grad_out, combine=combine, routes=routes, w_in=w_in, w_out=w_out)


def gelu_slope(preact):
    coeff = math.sqrt(2.0 / math.pi)
    inner = coeff * (preact + 0.044715 * preact * preact * preact)
    tanh_val = jnp.tanh(inner)
    return 0.5 * (1.0 + tanh_val) + 0.5 * preact * (1.0 - tanh_val * tanh_val) * coeff * (1.0 + 3.0 * 0.044715 * preact * preact)

def reference(hidden_in, grad_out, combine, routes, w_in, w_out):
    blocks = TOKENS // TOK_DEV
    flat_routes = routes.reshape(blocks, TOK_DEV * TOP)
    onehot = (flat_routes[:, :, None] == jnp.arange(EXPERTS, dtype=jnp.int32)[None, None, :]).astype(jnp.int32)
    earlier = jnp.cumsum(onehot, axis=1) - onehot
    slot_index = lax.optimization_barrier(jnp.sum(earlier * onehot, axis=2)).astype(jnp.int32)
    position = (flat_routes * CAP + slot_index).astype(jnp.int32)
    assign = (jnp.arange(TOK_DEV * TOP, dtype=jnp.int32)[None, :] + (jnp.arange(blocks, dtype=jnp.int32) * (TOK_DEV * TOP))[:, None]).astype(jnp.int32)
    slot_table = jnp.full((blocks, EXPERTS * CAP), TOKENS * TOP, jnp.int32)
    slot_table = slot_table.at[jnp.arange(blocks, dtype=jnp.int32)[:, None], position].set(assign)
    slot_table = slot_table.reshape(blocks, EXPERTS, CAP).transpose(1, 0, 2).reshape(EXPERTS, blocks * CAP)
    filled = slot_table < TOKENS * TOP
    safe_index = jnp.where(filled, slot_table, 0).astype(jnp.int32)
    token_index = (safe_index // TOP).astype(jnp.int32)
    rows_gate = jnp.where(filled, combine.reshape(-1)[safe_index], jnp.float32(0.0))

    def one_expert(packed):
        w_first, w_second, tok_rows, gate_rows = packed
        rows_x = hidden_in[tok_rows]
        rows_dy = grad_out[tok_rows]
        preact = jnp.dot(rows_x, w_first, preferred_element_type=jnp.float32)
        hidden = jax.nn.gelu(preact, approximate=True).astype(jnp.bfloat16)
        back_proj = jnp.dot(rows_dy, w_second.T, preferred_element_type=jnp.float32)
        gate_grad = lax.optimization_barrier(jnp.sum(hidden.astype(jnp.float32) * back_proj, axis=1))
        weighted = (gate_rows[:, None] * hidden.astype(jnp.float32)).astype(jnp.bfloat16)
        grad_second = jnp.dot(weighted.T, rows_dy, preferred_element_type=jnp.float32).astype(jnp.bfloat16)
        dpre = (gate_rows[:, None] * back_proj * gelu_slope(preact)).astype(jnp.bfloat16)
        grad_first = jnp.dot(rows_x.T, dpre, preferred_element_type=jnp.float32).astype(jnp.bfloat16)
        row_grad = jnp.dot(dpre, w_first.T, preferred_element_type=jnp.float32)
        return (grad_first, grad_second, row_grad, gate_grad)
    grad_w_in, grad_w_out, row_grads, gate_grads = lax.map(one_expert, (w_in, w_out, token_index, rows_gate))
    row_grads = jnp.where(filled.reshape(-1)[:, None], row_grads.reshape(-1, D), jnp.float32(0.0))
    grad_x = jnp.zeros((TOKENS, D), jnp.float32).at[token_index.reshape(-1)].add(row_grads).astype(jnp.bfloat16)
    target = jnp.where(filled, slot_table, TOKENS * TOP).astype(jnp.int32).reshape(-1)
    grad_combine = jnp.zeros((TOKENS * TOP,), jnp.float32).at[target].set(gate_grads.reshape(-1), mode='drop')
    return (grad_x, grad_combine.reshape(TOKENS, TOP), grad_w_in, grad_w_out)
```

```python
import functools
import math

import jax
import jax.numpy as jnp
from jax import lax
from jax.experimental import pallas as pl
from jax.experimental.pallas import tpu as pltpu
from jax.sharding import PartitionSpec as P

BF = jnp.bfloat16
F32 = jnp.float32
CHUNKS = (12, 8)
META = 16
LANES = 128
VMEM = 60 * 1024 * 1024


def mm(a, b, dims):
    return lax.dot_general(a, b, (dims, ((), ())), preferred_element_type=F32)


NN = ((1,), (0,))
NT = ((1,), (1,))
TN = ((0,), (0,))


def positions(names, experts):
    tokens = names.shape[1]
    expert = lax.broadcasted_iota(jnp.int32, (experts, tokens), 0).astype(F32)
    member = (names[0:1] == expert) | (names[1:2] == expert)
    first = lax.broadcasted_iota(jnp.int32, (tokens, tokens), 0)
    second = lax.broadcasted_iota(jnp.int32, (tokens, tokens), 1)
    earlier = jnp.where(first < second, 1.0, 0.0).astype(BF)
    count = mm(jnp.where(member, 1.0, 0.0).astype(BF), earlier, NN)
    return jnp.where(member, count, -1.0)


def row_owner(experts, span):
    rows = experts * span
    row = lax.broadcasted_iota(jnp.int32, (rows, experts), 0)
    expert = lax.broadcasted_iota(jnp.int32, (rows, experts), 1)
    own = (row >= expert * span) & (row < (expert + 1) * span)
    number = jnp.sum(jnp.where(own, expert, 0).astype(F32), axis=1, keepdims=True)
    slot = row[:, 0:1].astype(F32) - number * span
    return jnp.where(own, 1.0, 0.0).astype(BF), number, slot


def prep_kernel(experts, chunks, x_ref, dy_ref, names_ref, gates_ref, *outs):
    msg_ref, xs_ref = outs
    tokens, width = x_ref.shape
    names = names_ref[...].astype(F32)
    gates = gates_ref[...]
    high = gates.astype(BF).astype(F32)
    low = gates - high
    msg_ref[0:tokens, :] = dy_ref[...]
    line = lax.broadcasted_iota(jnp.int32, (META, tokens), 0)
    meta = jnp.zeros((META, tokens), F32)
    for at, part in enumerate((names, high, low)):
        for k in range(2):
            meta = jnp.where(line == 2 * at + k, part[k : k + 1], meta)
    msg_ref[tokens:, :] = jnp.zeros((META, width), BF)
    msg_ref[tokens:, 0:tokens] = meta.astype(BF)
    pos = positions(names, experts)
    span = sum(chunks)
    own, _, slot = row_owner(experts, span)
    picker = mm(own, pos.astype(BF), NN) == slot
    xs_ref[...] = mm(jnp.where(picker, 1.0, 0.0).astype(BF), x_ref[...], NN).astype(BF)


def expand_kernel(experts, chunks, *refs):
    blocks = len(refs) - len(chunks)
    msgs, outs = refs[:blocks], refs[blocks:]
    tokens = msgs[0].shape[0] - META
    dy = jnp.concatenate([m[0:tokens, :] for m in msgs], axis=0)
    expert = lax.broadcasted_iota(jnp.int32, (experts, tokens), 0).astype(F32)
    pos, gate = [], []
    for m in msgs:
        meta = m[tokens:, 0:tokens].astype(F32)
        pos.append(positions(meta[0:2], experts))
        both = meta[2:4] + meta[4:6]
        gate.append(
            jnp.where(meta[0:1] == expert, both[0:1], 0.0)
            + jnp.where(meta[1:2] == expert, both[1:2], 0.0)
        )
    gate = jnp.concatenate(gate, axis=1)
    high = gate.astype(BF)
    low = (gate - high.astype(F32)).astype(BF)
    base = 0
    for s, out in zip(chunks, outs):
        own, _, slot = row_owner(experts, blocks * s)
        here = jnp.concatenate(
            [
                jnp.where((p >= base) & (p < base + s), p - base + k * s, -1.0)
                for k, p in enumerate(pos)
            ],
            axis=1,
        )
        picker = mm(own, here.astype(BF), NN) == slot
        row_gate = jnp.sum(
            jnp.where(picker, mm(own, high, NN) + mm(own, low, NN), 0.0), axis=1, keepdims=True
        )
        rows = mm(jnp.where(picker, 1.0, 0.0).astype(BF), dy, NN)
        out[...] = (rows * row_gate).astype(BF)
        base += s


def rows_kernel(x_ref, dy_ref, wi_ref, wo_ref, hid_ref, dpre_ref, dx_ref):
    width = x_ref.shape[1]
    coeff = math.sqrt(2.0 / math.pi)
    pre = mm(wi_ref[...], x_ref[...], NT)
    back = mm(wo_ref[...], dy_ref[...], NT)
    square = pre * pre
    tanh = jnp.tanh(coeff * pre * (1.0 + 0.044715 * square))
    half = 0.5 * (1.0 + tanh)
    hidden = (pre * half).astype(BF)
    slope = half + 0.5 * coeff * pre * (1.0 - tanh * tanh) * (1.0 + 3.0 * 0.044715 * square)
    dpre = (back * slope).astype(BF)
    hid_ref[...] = hidden
    dpre_ref[...] = dpre
    prod = hidden.astype(F32) * back
    part = jnp.sum(prod.reshape(prod.shape[0] // 16, 16, prod.shape[1]), axis=0).astype(BF)
    line = lax.broadcasted_iota(jnp.int32, (16, LANES), 0)
    lane = lax.broadcasted_iota(jnp.int32, (16, LANES), 1)
    dx_ref[:, 0:width] = mm(dpre, wi_ref[...], TN).astype(BF)
    dx_ref[:, width:] = mm(part, jnp.where(line == lane, 1.0, 0.0).astype(BF), TN).astype(BF)


def weights_kernel(count, add, *refs):
    per = 4
    ins, rest = refs[: per * count], refs[per * count :]
    total_o = total_i = None
    for c in range(count):
        hid, dpre, x, dy = ins[per * c : per * c + per]
        part_o = mm(hid[...], dy[...], NN)
        part_i = mm(dpre[...], x[...], NN)
        total_o = part_o if c == 0 else total_o + part_o
        total_i = part_i if c == 0 else total_i + part_i
    if add:
        got_o, got_i, out_o, out_i = rest
        total_o = total_o + got_o[...].astype(F32)
        total_i = total_i + got_i[...].astype(F32)
    else:
        out_o, out_i = rest
    out_o[...] = total_o.astype(BF)
    out_i[...] = total_i.astype(BF)


def combine_kernel(experts, chunks, *refs):
    names_ref, gates_ref = refs[:2]
    rets = refs[2 : 2 + len(chunks)]
    dx_ref, gate_ref = refs[2 + len(chunks) :]
    width = dx_ref.shape[1]
    names = names_ref[...].astype(F32)
    pos = positions(names, experts)
    base, total = 0, None
    sums = [None, None]
    for s, ret in zip(chunks, rets):
        own, number, slot = row_owner(experts, s)
        here = jnp.where((pos >= base) & (pos < base + s), pos - base, -1.0)
        picker = mm(own, here.astype(BF), NN) == slot
        part = mm(jnp.where(picker, 1.0, 0.0).astype(BF), ret[:, 0:width], TN)
        total = part if total is None else total + part
        value = jnp.sum(ret[:, width:].astype(F32), axis=1, keepdims=True)
        for k in range(2):
            mine = jnp.sum(
                jnp.where(picker & (names[k : k + 1] == number), value, 0.0), axis=0, keepdims=True
            )
            sums[k] = mine if sums[k] is None else sums[k] + mine
        base += s
    dx_ref[...] = total.astype(BF)
    line = lax.broadcasted_iota(jnp.int32, gate_ref.shape, 0)
    gate_ref[...] = jnp.where(line == 0, sums[0], sums[1]) / gates_ref[...]


def call(kernel, outs, flops, moved, **more):
    return pl.pallas_call(
        kernel,
        out_shape=outs,
        compiler_params=pltpu.CompilerParams(vmem_limit_bytes=VMEM),
        cost_estimate=pl.CostEstimate(flops=int(flops), bytes_accessed=int(moved), transcendentals=0),
        **more,
    )


def shift(value, axis, by):
    size = lax.axis_size(axis)
    return lax.ppermute(value, axis, [(i, (i + by) % size) for i in range(size)])


def exchange(value):
    return lax.all_to_all(value, "expert", split_axis=0, concat_axis=0, tiled=True)


def local(hidden_in, grad_out, combine, routes, w_in, w_out):
    tokens, width = hidden_in.shape
    units = w_out.shape[1]
    experts = lax.axis_size("expert")
    planes = lax.axis_size("dp")
    cap = sum(CHUNKS)
    names, gates = routes.T, combine.T
    wi = w_in[0].T
    wo = w_out[0]
    wi = jnp.concatenate([wi, shift(wi, "seq", 1)], axis=0)
    wo = jnp.concatenate([wo, shift(wo, "seq", 1)], axis=0)
    hidden_units = 2 * units

    def arr(*shape, kind=BF):
        return jax.ShapeDtypeStruct(shape, kind)

    msg, xs = call(
        functools.partial(prep_kernel, experts, CHUNKS),
        [arr(tokens + META, width), arr(experts * cap, width)],
        2 * experts * cap * tokens * width,
        3e6,
    )(hidden_in, grad_out, names, gates)
    msgs = [msg] + [shift(msg, "dp", k) for k in range(1, planes)]
    xa = exchange(xs)
    xall = [xa] + [shift(xa, "dp", k) for k in range(1, planes)]
    sent = call(
        functools.partial(expand_kernel, experts, CHUNKS),
        [arr(experts * planes * s, width) for s in CHUNKS],
        2 * experts * planes * cap * planes * tokens * width,
        5e6,
    )(*msgs)
    base = 0
    done, rets = [], []
    for s, rows in zip(CHUNKS, sent):
        got = exchange(rows)
        got = got.reshape(experts, planes, s, width).swapaxes(0, 1)
        dy = got.reshape(planes * experts * s, width)
        x = jnp.concatenate(
            [
                v.reshape(experts, cap, width)[:, base : base + s].reshape(experts * s, width)
                for v in xall
            ],
            axis=0,
        )
        base += s
        count = x.shape[0]
        tile = 256
        hid, dpre, dx = call(
            rows_kernel,
            [arr(hidden_units, count), arr(hidden_units, count), arr(count, width + LANES)],
            6 * count * hidden_units * width,
            15e6,
            grid=(count // tile,),
            in_specs=[
                pl.BlockSpec((tile, width), lambda i: (i, 0)),
                pl.BlockSpec((tile, width), lambda i: (i, 0)),
                pl.BlockSpec((hidden_units, width), lambda i: (0, 0)),
                pl.BlockSpec((hidden_units, width), lambda i: (0, 0)),
            ],
            out_specs=[
                pl.BlockSpec((hidden_units, tile), lambda i: (0, i)),
                pl.BlockSpec((hidden_units, tile), lambda i: (0, i)),
                pl.BlockSpec((tile, width + LANES), lambda i: (i, 0)),
            ],
        )(x, dy, wi, wo)
        done.append((hid, dpre, x, dy))
        block = experts * s
        own = dx[0:block].astype(F32)
        for k in range(1, planes):
            own = own + shift(dx[k * block : (k + 1) * block], "dp", -k).astype(F32)
        rets.append(exchange(own.astype(BF)))

    def weight_call(half, extra):
        tiles = 2
        size = units // tiles
        specs, args = [], []
        for hid, dpre, x, dy in done:
            count = x.shape[0]
            specs += [pl.BlockSpec((size, count), lambda i: (half * tiles + i, 0))] * 2
            specs += [pl.BlockSpec((count, width), lambda i: (0, 0))] * 2
            args += [hid, dpre, x, dy]
        block = pl.BlockSpec((size, width), lambda i: (i, 0))
        return call(
            functools.partial(weights_kernel, len(done), bool(extra)),
            [arr(units, width), arr(units, width)],
            4 * units * width * planes * experts * cap,
            12e6,
            grid=(tiles,),
            in_specs=specs + [block] * len(extra),
            out_specs=[block, block],
        )(*args, *extra)

    theirs = weight_call(1, ())
    received = [shift(v, "seq", 1) for v in theirs]
    grad_wo, grad_wi = weight_call(0, tuple(received))
    grad_x, grad_gate = call(
        functools.partial(combine_kernel, experts, CHUNKS),
        [arr(tokens, width), arr(2, tokens, kind=F32)],
        2 * experts * cap * tokens * width,
        2e6,
    )(names, gates, *rets)
    return grad_x, grad_gate.T, grad_wi.T[None], grad_wo[None]


def solution(mesh):
    rows = P(("dp", "seq", "expert"), None)
    first = P("expert", None, ("dp", "seq"))
    second = P("expert", ("dp", "seq"), None)
    return jax.shard_map(
        local,
        mesh=mesh,
        in_specs=(rows, rows, rows, rows, first, second),
        out_specs=(rows, rows, first, second),
        check_vma=False,
    )
```

```python
import functools
import math

import jax
import jax.numpy as jnp
from jax import lax
from jax.experimental import pallas as pl
from jax.experimental.pallas import tpu as pltpu
from jax.sharding import PartitionSpec as P

BF = jnp.bfloat16
F32 = jnp.float32
CHUNKS = (12, 8)
META = 16
LANES = 128
HBM = pl.BlockSpec(memory_space=pltpu.HBM)
MIB = 1024 * 1024


def mm(a, b, dims):
    return lax.dot_general(a, b, (dims, ((), ())), preferred_element_type=F32)


def ones(mask):
    return jnp.where(mask, 1.0, 0.0).astype(BF)


def eights(count):
    return -(-count // 8) * 8


NN = ((1,), (0,))
NT = ((1,), (1,))
TN = ((0,), (0,))


def positions(names, experts):
    tokens = names.shape[1]
    expert = lax.broadcasted_iota(jnp.int32, (experts, tokens), 0).astype(F32)
    member = (names[0:1] == expert) | (names[1:2] == expert)
    first = lax.broadcasted_iota(jnp.int32, (tokens, tokens), 0)
    second = lax.broadcasted_iota(jnp.int32, (tokens, tokens), 1)
    earlier = jnp.where(first < second, 1.0, 0.0).astype(BF)
    count = mm(jnp.where(member, 1.0, 0.0).astype(BF), earlier, NN)
    return jnp.where(member, count, -1.0)


def row_owner(experts, span):
    rows = experts * span
    row = lax.broadcasted_iota(jnp.int32, (rows, experts), 0)
    expert = lax.broadcasted_iota(jnp.int32, (rows, experts), 1)
    own = (row >= expert * span) & (row < (expert + 1) * span)
    number = jnp.sum(jnp.where(own, expert, 0).astype(F32), axis=1, keepdims=True)
    slot = row[:, 0:1].astype(F32) - number * span
    return jnp.where(own, 1.0, 0.0).astype(BF), number, slot


def message_kernel(dy_ref, names_ref, gates_ref, msg_ref):
    tokens, width = dy_ref.shape
    names = names_ref[...].astype(F32)
    gates = gates_ref[...]
    high = gates.astype(BF).astype(F32)
    low = gates - high
    msg_ref[0:tokens, :] = dy_ref[...]
    line = lax.broadcasted_iota(jnp.int32, (META, tokens), 0)
    meta = jnp.zeros((META, tokens), F32)
    for at, part in enumerate((names, high, low)):
        for k in range(2):
            meta = jnp.where(line == 2 * at + k, part[k : k + 1], meta)
    msg_ref[tokens:, :] = jnp.zeros((META, width), BF)
    msg_ref[tokens:, 0:tokens] = meta.astype(BF)


def pick_kernel(experts, x_ref, names_ref, xs_ref):
    pos = positions(names_ref[...].astype(F32), experts)
    own, _, slot = row_owner(experts, xs_ref.shape[0] // experts)
    picker = mm(own, pos.astype(BF), NN) == slot
    xs_ref[...] = mm(ones(picker), x_ref[...], NN).astype(BF)


def expand_kernel(experts, base, s, *refs):
    msgs, out = refs[:-1], refs[-1]
    blocks = len(msgs)
    tokens = msgs[0].shape[0] - META
    dy = jnp.concatenate([m[0:tokens, :] for m in msgs], axis=0)
    expert = lax.broadcasted_iota(jnp.int32, (experts, tokens), 0).astype(F32)
    here, gate = [], []
    for k, m in enumerate(msgs):
        meta = m[tokens:, 0:tokens].astype(F32)
        p = positions(meta[0:2], experts)
        here.append(jnp.where((p >= base) & (p < base + s), p - base + k * s, -1.0))
        both = meta[2:4] + meta[4:6]
        gate.append(
            jnp.where(meta[0:1] == expert, both[0:1], 0.0)
            + jnp.where(meta[1:2] == expert, both[1:2], 0.0)
        )
    gate = jnp.concatenate(gate, axis=1)
    here = jnp.concatenate(here, axis=1)
    high = gate.astype(BF)
    low = (gate - high.astype(F32)).astype(BF)
    own, _, slot = row_owner(experts, blocks * s)
    picker = mm(own, here.astype(BF), NN) == slot
    row_gate = jnp.sum(
        jnp.where(picker, mm(own, high, NN) + mm(own, low, NN), 0.0), axis=1, keepdims=True
    )
    out[...] = (mm(ones(picker), dy, NN) * row_gate).astype(BF)


def regroup(experts, span, base, count):
    _, number, slot = row_owner(experts, span)
    inside = (slot >= base) & (slot < base + count)
    want = jnp.where(inside, number * count + (slot - base), -1.0)
    shape = (experts * span, experts * count)
    return ones(lax.broadcasted_iota(jnp.int32, shape, 1).astype(F32) == want)


def gather(experts, count, span, base):
    _, number, slot = row_owner(experts, count)
    want = number * span + (base + slot)
    shape = (experts * count, experts * span)
    return ones(lax.broadcasted_iota(jnp.int32, shape, 1).astype(F32) == want)


def split_kernel(experts, chunks, got_ref, out_ref):
    span = got_ref.shape[0] // experts
    base = 0
    for s in chunks:
        rows = pl.ds(base * experts, s * experts)
        out_ref[rows, :] = mm(gather(experts, s, span, base), got_ref[...], NN).astype(BF)
        base += s


def rows_kernel(experts, blocks, base, s, *refs):
    xs, rest = refs[:blocks], refs[blocks:]
    got_ref, wi_mine, wi_other, wo_mine, wo_other, hid_out, dpre_out, dy_out = rest[:8]
    dxs, rest = rest[8 : 8 + blocks], rest[8 + blocks :]
    x_ref, got, dy_ref, wi_ref, wo_ref, hid_ref, dpre_ref, dx_ref, sems = rest
    width = x_ref.shape[1]
    block = experts * s
    units = wi_mine.shape[0]
    coeff = math.sqrt(2.0 / math.pi)
    copies = []

    def start(source, target):
        copies.append(pltpu.make_async_copy(source, target, sems.at[len(copies)]))
        copies[-1].start()
        return copies[-1]

    first = [start(got_ref, got)]
    second = [
        start(x.at[pl.ds(base * experts, block)], x_ref.at[pl.ds(k * block, block)])
        for k, x in enumerate(xs)
    ]
    for weight, mine, other in ((wi_ref, wi_mine, wi_other), (wo_ref, wo_mine, wo_other)):
        second.append(start(mine, weight.at[pl.ds(0, units)]))
        second.append(start(other, weight.at[pl.ds(units, units)]))
    for c in first:
        c.wait()
    for k in range(blocks):
        take = gather(experts, s, blocks * s, k * s)
        dy_ref[pl.ds(k * block, block), :] = mm(take, got[...], NN).astype(BF)
    for c in second:
        c.wait()
    last = [start(dy_ref, dy_out)]
    line = lax.broadcasted_iota(jnp.int32, (16, LANES), 0)
    lane = lax.broadcasted_iota(jnp.int32, (16, LANES), 1)
    tile = 256
    for at in range(0, blocks * block, tile):
        pre = mm(wi_ref[...], x_ref[at : at + tile, :], NT)
        back = mm(wo_ref[...], dy_ref[at : at + tile, :], NT)
        square = pre * pre
        tanh = jnp.tanh(coeff * pre * (1.0 + 0.044715 * square))
        half = 0.5 * (1.0 + tanh)
        hidden = (pre * half).astype(BF)
        slope = half + 0.5 * coeff * pre * (1.0 - tanh * tanh) * (1.0 + 3.0 * 0.044715 * square)
        hid_ref[:, at : at + tile] = hidden
        dpre_ref[:, at : at + tile] = (back * slope).astype(BF)
        prod = hidden.astype(F32) * back
        part = jnp.sum(prod.reshape(prod.shape[0] // 16, 16, tile), axis=0).astype(BF)
        dx_ref[at : at + tile, width:] = mm(part, ones(line == lane), TN).astype(BF)
        last.append(start(hid_ref.at[:, pl.ds(at, tile)], hid_out.at[:, pl.ds(at, tile)]))
        last.append(start(dpre_ref.at[:, pl.ds(at, tile)], dpre_out.at[:, pl.ds(at, tile)]))
    dx_ref[:, 0:width] = mm(dpre_ref[...], wi_ref[...], TN).astype(BF)
    for k in range(blocks):
        last.append(start(dx_ref.at[pl.ds(k * block, block)], dxs[k]))
    for c in last:
        c.wait()


def add_kernel(experts, blocks, chunks, *refs):
    out, base, laid = refs[-1], 0, None
    span = out.shape[0] // experts
    for c, s in enumerate(chunks):
        total = None
        for r in refs[c * blocks : (c + 1) * blocks]:
            part = r[...].astype(F32)
            total = part if total is None else total + part
        part = mm(regroup(experts, span, base, s), total.astype(BF), NN)
        laid = part if laid is None else laid + part
        base += s
    out[...] = laid.astype(BF)


def weights_kernel(blocks, first, *refs):
    hid, dpre, dy, *refs = refs
    xs, refs = refs[:blocks], refs[blocks:]
    held_hid, held_dpre, held_dy, held_x, out_o, out_i, out_other, sems = refs[-8:]
    outs, earlier = refs[-11:-8], refs[:-11]
    stored = (out_o, out_i, out_other)
    units = out_o.shape[0]
    copies = []

    def start(source, target):
        copies.append(pltpu.make_async_copy(source, target, sems.at[len(copies)]))
        copies[-1].start()
        return copies[-1]

    rows = held_x.shape[0] // blocks
    waits = [
        [start(hid, held_hid), start(dy, held_dy)],
        [start(dpre, held_dpre)]
        + [
            start(x.at[pl.ds(first, rows)], held_x.at[pl.ds(k * rows, rows)])
            for k, x in enumerate(xs)
        ],
    ]
    before = [start(e, s) for e, s in zip(earlier, stored)]
    last = []
    for which, (left, right) in enumerate(((held_hid, held_dy), (held_dpre, held_x))):
        for w in waits[which]:
            w.wait()
        for half in (1, 0):
            part = mm(left[pl.ds(half * units, units), :], right[...], NN)
            spot = pl.ds(which * units if half else 0, units)
            target = 2 if half else which
            if before:
                if which == 0 and half:
                    before[2].wait()
                if not half:
                    before[which].wait()
                part = part + stored[target][spot, :].astype(F32)
            stored[target][spot, :] = part.astype(BF)
            last.append(start(stored[target].at[spot], outs[target].at[spot]))
    for c in last:
        c.wait()


def combine_kernel(experts, names_ref, gates_ref, ret_ref, dx_ref, gate_ref):
    width = dx_ref.shape[1]
    names = names_ref[...].astype(F32)
    pos = positions(names, experts)
    own, number, slot = row_owner(experts, ret_ref.shape[0] // experts)
    picker = mm(own, pos.astype(BF), NN) == slot
    dx_ref[...] = mm(ones(picker), ret_ref[:, 0:width], TN).astype(BF)
    value = jnp.sum(ret_ref[:, width:].astype(F32), axis=1, keepdims=True)
    sums = [
        jnp.sum(jnp.where(picker & (names[k : k + 1] == number), value, 0.0), axis=0, keepdims=True)
        for k in range(2)
    ]
    line = lax.broadcasted_iota(jnp.int32, gate_ref.shape, 0)
    gate_ref[...] = jnp.where(line == 0, sums[0], sums[1]) / gates_ref[...]


def call(kernel, outs, flops, moved, **more):
    return pl.pallas_call(
        kernel,
        out_shape=outs,
        compiler_params=pltpu.CompilerParams(vmem_limit_bytes=60 * MIB),
        cost_estimate=pl.CostEstimate(flops=1, bytes_accessed=1, transcendentals=0),
        **more,
    )


def shift(value, axis, by):
    size = lax.axis_size(axis)
    return lax.ppermute(value, axis, [(i, (i + by) % size) for i in range(size)])


def exchange(value):
    return lax.all_to_all(value, "expert", split_axis=0, concat_axis=0, tiled=True)


def local(hidden_in, grad_out, combine, routes, w_in, w_out):
    tokens, width = hidden_in.shape
    units = w_out.shape[1]
    experts = lax.axis_size("expert")
    planes = lax.axis_size("dp")
    cap = sum(CHUNKS)
    names, gates = routes.T, combine.T
    wi, wo = w_in[0].T, w_out[0]
    hidden_units = 2 * units
    after = lax.optimization_barrier

    def arr(*shape, kind=BF):
        return jax.ShapeDtypeStruct(shape, kind)

    def ring(value, sign):
        return [shift(v, "dp", sign * k) for k, v in enumerate(value, 1)]

    msg = call(message_kernel, arr(tokens + META, width), 1e5, 6e5)(grad_out, names, gates)
    msgs = [msg] + ring([msg] * (planes - 1), 1)
    xs = call(
        functools.partial(pick_kernel, experts),
        arr(experts * eights(cap), width),
        2 * experts * cap * tokens * width,
        1e6,
    )(hidden_in, names)
    wi_other, wo_other = shift(wi, "seq", 1), shift(wo, "seq", 1)
    msgs, wi_other, wo_other = after((msgs, wi_other, wo_other))
    sent, base = [], 0
    for s in CHUNKS:
        count = planes * experts * s
        sent.append(
            call(
                functools.partial(expand_kernel, experts, base, s),
                arr(count, width),
                2 * count * planes * tokens * width,
                3e6,
            )(*msgs)
        )
        base += s
    xa = exchange(xs)
    xa = call(
        functools.partial(split_kernel, experts, CHUNKS),
        arr(experts * cap, width),
        2 * (experts * cap) ** 2 * width,
        2e6,
    )(xa)
    x = [xa] + ring([xa] * (planes - 1), 1)
    sent[0], xa = after((sent[0], xa))
    got = exchange(sent[0])
    sent[1], got = after((sent[1], got))
    got = [got, exchange(sent[1])]

    def rows_call(c):
        block = experts * CHUNKS[c]
        count = planes * block
        hid, dpre, dy, *dx = call(
            functools.partial(rows_kernel, experts, planes, sum(CHUNKS[:c]), CHUNKS[c]),
            [arr(hidden_units, count)] * 2
            + [arr(count, width)]
            + [arr(block, width + LANES)] * planes,
            6 * count * hidden_units * width,
            15e6,
            in_specs=[HBM] * (planes + 5),
            out_specs=[HBM] * (planes + 3),
            scratch_shapes=[pltpu.VMEM((count, width), BF)] * 3
            + [pltpu.VMEM((hidden_units, width), BF)] * 2
            + [pltpu.VMEM((hidden_units, count), BF)] * 2
            + [pltpu.VMEM((count, width + LANES), BF), pltpu.SemaphoreType.DMA((32,))],
        )(*x, got[c], wi, wi_other, wo, wo_other)
        return [hid, dpre, dy, *x], dx

    def weights_call(c, done, earlier):
        count = done[2].shape[0]
        grads = [(units, width)] * 2 + [(2 * units, width)]
        return call(
            functools.partial(weights_kernel, planes, experts * sum(CHUNKS[:c])),
            [arr(*g) for g in grads],
            4 * hidden_units * width * count,
            15e6,
            in_specs=[HBM] * (len(done) + len(earlier)),
            out_specs=[HBM] * 3,
            scratch_shapes=[pltpu.VMEM((hidden_units, count), BF)] * 2
            + [pltpu.VMEM((count, width), BF)] * 2
            + [pltpu.VMEM(g, BF) for g in grads]
            + [pltpu.SemaphoreType.DMA((32,))],
        )(*done, *earlier)

    done1, dx1 = rows_call(0)
    dx1[1:] = ring(dx1[1:], -1)
    grads = weights_call(0, done1, [])
    got[1], grads = after((got[1], grads))
    done2, dx2 = rows_call(1)
    dx2[1:] = ring(dx2[1:], -1)
    grads = weights_call(1, done2, grads)
    dx1, dx2, grads = after((dx1, dx2, grads))
    back = call(
        functools.partial(add_kernel, experts, planes, CHUNKS),
        arr(experts * eights(cap), width + LANES),
        1e6,
        6e6,
    )(*dx1, *dx2)
    mine_o, mine_i, theirs = grads
    theirs = shift(theirs, "seq", 1).astype(F32)
    grad_wo = (mine_o.astype(F32) + theirs[:units]).astype(BF)
    grad_wi = (mine_i.astype(F32) + theirs[units:]).astype(BF)
    back, grad_wo, grad_wi = after((exchange(back), grad_wo, grad_wi))
    grad_x, grad_gate = call(
        functools.partial(combine_kernel, experts),
        [arr(tokens, width), arr(2, tokens, kind=F32)],
        2 * experts * cap * tokens * width,
        2e6,
    )(names, gates, back)
    return grad_x, grad_gate.T, grad_wi.T[None], grad_wo[None]


def solution(mesh):
    rows = P(("dp", "seq", "expert"), None)
    first = P("expert", None, ("dp", "seq"))
    second = P("expert", ("dp", "seq"), None)
    return jax.shard_map(
        local,
        mesh=mesh,
        in_specs=(rows, rows, rows, rows, first, second),
        out_specs=(rows, rows, first, second),
        check_vma=False,
    )
```

```python
import functools
import math

import jax
import jax.numpy as jnp
from jax import lax
from jax.experimental import pallas as pl
from jax.experimental.pallas import tpu as pltpu
from jax.sharding import PartitionSpec as P

BF = jnp.bfloat16
F32 = jnp.float32
CAP = 20
GROUPS = ((1, 3), (2, 0))
META = 16
LANES = 128
HBM = pl.BlockSpec(memory_space=pltpu.HBM)
SMALL, LARGE = 12, 60
MIB = 1024 * 1024


def mm(a, b, dims):
    return lax.dot_general(a, b, (dims, ((), ())), preferred_element_type=F32)


def ones(mask):
    return jnp.where(mask, 1.0, 0.0).astype(BF)


def eights(count):
    return -(-count // 8) * 8


NN = ((1,), (0,))
NT = ((1,), (1,))
TN = ((0,), (0,))


def positions(names, experts):
    tokens = names.shape[1]
    expert = lax.broadcasted_iota(jnp.int32, (experts, tokens), 0).astype(F32)
    member = (names[0:1] == expert) | (names[1:2] == expert)
    first = lax.broadcasted_iota(jnp.int32, (tokens, tokens), 0)
    second = lax.broadcasted_iota(jnp.int32, (tokens, tokens), 1)
    earlier = jnp.where(first < second, 1.0, 0.0).astype(BF)
    count = mm(jnp.where(member, 1.0, 0.0).astype(BF), earlier, NN)
    return jnp.where(member, count, -1.0)


def row_owner(experts, span):
    rows = experts * span
    row = lax.broadcasted_iota(jnp.int32, (rows, experts), 0)
    expert = lax.broadcasted_iota(jnp.int32, (rows, experts), 1)
    own = (row >= expert * span) & (row < (expert + 1) * span)
    number = jnp.sum(jnp.where(own, expert, 0).astype(F32), axis=1, keepdims=True)
    slot = row[:, 0:1].astype(F32) - number * span
    return jnp.where(own, 1.0, 0.0).astype(BF), number, slot


def message_kernel(dy_ref, names_ref, gates_ref, msg_ref):
    tokens, width = dy_ref.shape
    names = names_ref[...].astype(F32)
    gates = gates_ref[...]
    high = gates.astype(BF).astype(F32)
    low = gates - high
    msg_ref[0:tokens, :] = dy_ref[...]
    line = lax.broadcasted_iota(jnp.int32, (META, tokens), 0)
    meta = jnp.zeros((META, tokens), F32)
    for at, part in enumerate((names, high, low)):
        for k in range(2):
            meta = jnp.where(line == 2 * at + k, part[k : k + 1], meta)
    msg_ref[tokens:, :] = jnp.zeros((META, width), BF)
    msg_ref[tokens:, 0:tokens] = meta.astype(BF)


def token_gates(names, gates, experts):
    expert = lax.broadcasted_iota(jnp.int32, (experts, names.shape[1]), 0).astype(F32)
    gate = jnp.where(names[0:1] == expert, gates[0:1], 0.0)
    gate = gate + jnp.where(names[1:2] == expert, gates[1:2], 0.0)
    high = gate.astype(BF)
    return high, (gate - high.astype(F32)).astype(BF)


def pick_kernel(experts, x_ref, names_ref, xs_ref):
    pos = positions(names_ref[...].astype(F32), experts)
    own, _, slot = row_owner(experts, xs_ref.shape[0] // experts)
    picker = mm(own, pos.astype(BF), NN) == slot
    xs_ref[...] = mm(ones(picker), x_ref[...], NN).astype(BF)


def expand_kernel(experts, cap, *refs):
    msgs, out = refs[:-1], refs[-1]
    tokens = msgs[0].shape[0] - META
    dy = jnp.concatenate([m[0:tokens, :] for m in msgs], axis=0)
    here, high, low = [], [], []
    for k, m in enumerate(msgs):
        meta = m[tokens:, 0:tokens].astype(F32)
        p = positions(meta[0:2], experts)
        here.append(jnp.where(p >= 0.0, p + k * cap, -1.0))
        parts = token_gates(meta[0:2], meta[2:4] + meta[4:6], experts)
        high.append(parts[0])
        low.append(parts[1])
    here, high, low = (jnp.concatenate(v, axis=1) for v in (here, high, low))
    own, _, slot = row_owner(experts, out.shape[0] // experts)
    picker = mm(own, here.astype(BF), NN) == slot
    gate = jnp.where(picker, mm(own, high, NN) + mm(own, low, NN), 0.0)
    gate = jnp.sum(gate, axis=1, keepdims=True)
    out[...] = (mm(ones(picker), dy, NN) * gate).astype(BF)


def regroup(experts, span, count):
    _, number, slot = row_owner(experts, span)
    want = jnp.where(slot < count, number * count + slot, -1.0)
    shape = (experts * span, experts * count)
    return ones(lax.broadcasted_iota(jnp.int32, shape, 1).astype(F32) == want)


def gather(experts, count, span, base):
    _, number, slot = row_owner(experts, count)
    want = number * span + (base + slot)
    shape = (experts * count, experts * span)
    return ones(lax.broadcasted_iota(jnp.int32, shape, 1).astype(F32) == want)


def split_kernel(experts, got_ref, out_ref):
    take = gather(experts, out_ref.shape[0] // experts, got_ref.shape[0] // experts, 0)
    out_ref[...] = mm(take, got_ref[...], NN).astype(BF)


def fill(start, parts, target):
    at, started = 0, []
    for part in parts:
        rows = part.shape[0]
        started.append(start(part, target.at[pl.ds(at, rows)]))
        at += rows
    return started


def rows_kernel(experts, parts, blocks, *refs):
    xs, refs = refs[:parts], refs[parts:]
    got_ref, wi_mine, wi_other, wo_mine, wo_other = refs[:5]
    hid_out, dpre_out, dy_out, *dxs = refs[5 : 8 + blocks]
    x_ref, got, dy_ref, wi_ref, wo_ref, hid_ref, dpre_ref, dx_ref, sems = refs[8 + blocks :]
    width = x_ref.shape[1]
    count = x_ref.shape[0]
    block = count // blocks
    units = wi_mine.shape[0]
    coeff = math.sqrt(2.0 / math.pi)
    copies = []

    def start(source, target):
        copies.append(pltpu.make_async_copy(source, target, sems.at[len(copies)]))
        copies[-1].start()
        return copies[-1]

    first = [start(got_ref, got)]
    second = fill(start, xs, x_ref)
    for weight, mine, other in ((wi_ref, wi_mine, wi_other), (wo_ref, wo_mine, wo_other)):
        second.append(start(mine, weight.at[pl.ds(0, units)]))
        second.append(start(other, weight.at[pl.ds(units, units)]))
    for c in first:
        c.wait()
    cap = block // experts
    for j in range(blocks):
        take = gather(experts, cap, blocks * cap, j * cap)
        dy_ref[pl.ds(j * block, block), :] = mm(take, got[...], NN).astype(BF)
    for c in second:
        c.wait()
    last = [start(dy_ref, dy_out)]
    line = lax.broadcasted_iota(jnp.int32, (16, LANES), 0)
    lane = lax.broadcasted_iota(jnp.int32, (16, LANES), 1)
    at = 0
    while at < count:
        tile = min(256, count - at)
        pre = mm(wi_ref[...], x_ref[at : at + tile, :], NT)
        back = mm(wo_ref[...], dy_ref[at : at + tile, :], NT)
        square = pre * pre
        tanh = jnp.tanh(coeff * pre * (1.0 + 0.044715 * square))
        half = 0.5 * (1.0 + tanh)
        hidden = (pre * half).astype(BF)
        slope = half + 0.5 * coeff * pre * (1.0 - tanh * tanh) * (1.0 + 3.0 * 0.044715 * square)
        hid_ref[:, at : at + tile] = hidden
        dpre_ref[:, at : at + tile] = (back * slope).astype(BF)
        prod = hidden.astype(F32) * back
        part = jnp.sum(prod.reshape(prod.shape[0] // 16, 16, tile), axis=0).astype(BF)
        dx_ref[at : at + tile, width:] = mm(part, ones(line == lane), TN).astype(BF)
        last.append(start(hid_ref.at[:, pl.ds(at, tile)], hid_out.at[:, pl.ds(at, tile)]))
        last.append(start(dpre_ref.at[:, pl.ds(at, tile)], dpre_out.at[:, pl.ds(at, tile)]))
        at += tile
    dx_ref[:, 0:width] = mm(dpre_ref[...], wi_ref[...], TN).astype(BF)
    for j in range(blocks):
        last.append(start(dx_ref.at[pl.ds(j * block, block)], dxs[j]))
    for c in last:
        c.wait()


def add_kernel(experts, *refs):
    total = refs[0][...].astype(F32)
    for r in refs[1:-1]:
        total = total + r[...].astype(F32)
    out = refs[-1]
    lay = regroup(experts, out.shape[0] // experts, total.shape[0] // experts)
    out[...] = mm(lay, total.astype(BF), NN).astype(BF)


def weights_kernel(groups, parts, *refs):
    ins, xs, refs = refs[: 3 * groups], refs[3 * groups :][:parts], refs[3 * groups + parts :]
    outs, (held_hid, held_dpre, held_dy, held_x), stored, sems = refs[:3], refs[3:7], refs[7:10], refs[10]
    units = stored[0].shape[0]
    copies = []

    def start(source, target):
        copies.append(pltpu.make_async_copy(source, target, sems.at[len(copies)]))
        copies[-1].start()
        return copies[-1]

    def columns(which, target):
        at, started = 0, []
        for part in ins[which::3]:
            count = part.shape[1]
            started.append(start(part, target.at[:, pl.ds(at, count)]))
            at += count
        return started

    waits = [columns(0, held_hid) + fill(start, ins[2::3], held_dy)]
    waits.append(columns(1, held_dpre) + fill(start, xs, held_x))
    last = []
    for which, (left, right) in enumerate(((held_hid, held_dy), (held_dpre, held_x))):
        for w in waits[which]:
            w.wait()
        for half in (1, 0):
            part = mm(left[pl.ds(half * units, units), :], right[...], NN).astype(BF)
            spot = pl.ds(which * units if half else 0, units)
            target = 2 if half else which
            stored[target][spot, :] = part
            last.append(start(stored[target].at[spot], outs[target].at[spot]))
    for c in last:
        c.wait()


def combine_kernel(experts, names_ref, gates_ref, ret_ref, dx_ref, gate_ref):
    width = dx_ref.shape[1]
    names = names_ref[...].astype(F32)
    pos = positions(names, experts)
    own, number, slot = row_owner(experts, ret_ref.shape[0] // experts)
    picker = mm(own, pos.astype(BF), NN) == slot
    dx_ref[...] = mm(ones(picker), ret_ref[:, 0:width], TN).astype(BF)
    value = jnp.sum(ret_ref[:, width:].astype(F32), axis=1, keepdims=True)
    sums = [
        jnp.sum(jnp.where(picker & (names[k : k + 1] == number), value, 0.0), axis=0, keepdims=True)
        for k in range(2)
    ]
    line = lax.broadcasted_iota(jnp.int32, gate_ref.shape, 0)
    gate_ref[...] = jnp.where(line == 0, sums[0], sums[1]) / gates_ref[...]


def call(kernel, outs, vmem, **more):
    return pl.pallas_call(
        kernel,
        out_shape=outs,
        compiler_params=pltpu.CompilerParams(vmem_limit_bytes=vmem * MIB),
        cost_estimate=pl.CostEstimate(flops=1, bytes_accessed=1, transcendentals=0),
        **more,
    )


def shift(value, axis, by):
    size = lax.axis_size(axis)
    return lax.ppermute(value, axis, [(i, (i + by) % size) for i in range(size)])


def exchange(value):
    return lax.all_to_all(value, "expert", split_axis=0, concat_axis=0, tiled=True)


def local(hidden_in, grad_out, combine, routes, w_in, w_out):
    tokens, width = hidden_in.shape
    units = w_out.shape[1]
    experts = lax.axis_size("expert")
    planes = lax.axis_size("dp")
    names, gates = routes.T, combine.T
    wi, wo = w_in[0].T, w_out[0]
    hidden_units = 2 * units
    block = experts * CAP
    after = lax.optimization_barrier

    def arr(*shape, kind=BF):
        return jax.ShapeDtypeStruct(shape, kind)

    msg = call(message_kernel, arr(tokens + META, width), SMALL)(grad_out, names, gates)
    msgs = {0: msg}
    for k in (1, 3, 2):
        msgs[k] = shift(msg, "dp", k)
    xs = call(functools.partial(pick_kernel, experts), arr(experts * eights(CAP), width), SMALL)(
        hidden_in, names
    )
    wi_other, wo_other = shift(wi, "seq", 1), shift(wo, "seq", 1)
    msgs[1], wi_other, wo_other = after((msgs[1], wi_other, wo_other))
    xa, msgs[1], msgs[3] = after((exchange(xs), msgs[1], msgs[3]))
    x = call(functools.partial(split_kernel, experts), arr(block, width), SMALL)(xa)
    x, msgs[1] = after((x, msgs[1]))
    half = block // 2
    near = [shift(x, "dp", 1), shift(x, "dp", -1)]
    def expand(g):
        return call(
            functools.partial(expand_kernel, experts, CAP),
            arr(block * len(GROUPS[g]), width),
            SMALL,
        )(*(msgs[k] for k in GROUPS[g]))

    sent, msgs[2] = after((expand(0), msgs[2]))
    got = exchange(sent)
    sent, got, near = after((expand(1), got, near))
    got = [got, exchange(sent)]
    xs = {0: [x], 1: near[:1], 3: near[1:]}
    xs[2] = [shift(xs[1][0][:half], "dp", 1), shift(xs[3][0][half:], "dp", -1)]

    def rows_call(g):
        blocks = len(GROUPS[g])
        count = blocks * block
        parts = sum((xs[k] for k in GROUPS[g]), [])
        hid, dpre, dy, *dx = call(
            functools.partial(rows_kernel, experts, len(parts), blocks),
            [arr(hidden_units, count)] * 2
            + [arr(count, width)]
            + [arr(block, width + LANES)] * blocks,
            LARGE,
            in_specs=[HBM] * (len(parts) + 5),
            out_specs=[HBM] * (3 + blocks),
            scratch_shapes=[pltpu.VMEM((count, width), BF)] * 3
            + [pltpu.VMEM((hidden_units, width), BF)] * 2
            + [pltpu.VMEM((hidden_units, count), BF)] * 2
            + [pltpu.VMEM((count, width + LANES), BF), pltpu.SemaphoreType.DMA((32,))],
        )(*parts, got[g], wi, wi_other, wo, wo_other)
        return [hid, dpre, dy], parts, dict(zip(GROUPS[g], dx))

    done_a, parts_a, dx = rows_call(0)
    dx = {k: shift(v, "dp", -k) for k, v in dx.items()}
    done_b, parts_b, dx_b = rows_call(1)
    dx[0], dx[2] = dx_b[0], shift(dx_b[2], "dp", 2)
    grads = [(units, width)] * 2 + [(2 * units, width)]
    total = planes * block
    ins = done_a + done_b + parts_a + parts_b
    mine_o, mine_i, theirs = call(
        functools.partial(weights_kernel, len(GROUPS), len(parts_a + parts_b)),
        [arr(*g) for g in grads],
        LARGE,
        in_specs=[HBM] * len(ins),
        out_specs=[HBM] * 3,
        scratch_shapes=[pltpu.VMEM((hidden_units, total), BF)] * 2
        + [pltpu.VMEM((total, width), BF)] * 2
        + [pltpu.VMEM(g, BF) for g in grads]
        + [pltpu.SemaphoreType.DMA((32,))],
    )(*ins)
    dx, theirs = after((dx, theirs))
    back = call(
        functools.partial(add_kernel, experts), arr(experts * eights(CAP), width + LANES), SMALL
    )(*(dx[k] for k in range(planes)))
    theirs = shift(theirs, "seq", 1).astype(F32)
    grad_wo = (mine_o.astype(F32) + theirs[:units]).astype(BF)
    grad_wi = (mine_i.astype(F32) + theirs[units:]).astype(BF)
    back, grad_wo, grad_wi = after((exchange(back), grad_wo, grad_wi))
    grad_x, grad_gate = call(
        functools.partial(combine_kernel, experts),
        [arr(tokens, width), arr(2, tokens, kind=F32)],
        SMALL,
    )(names, gates, back)
    return grad_x, grad_gate.T, grad_wi.T[None], grad_wo[None]


def solution(mesh):
    rows = P(("dp", "seq", "expert"), None)
    first = P("expert", None, ("dp", "seq"))
    second = P("expert", ("dp", "seq"), None)
    return jax.shard_map(
        local,
        mesh=mesh,
        in_specs=(rows, rows, rows, rows, first, second),
        out_specs=(rows, rows, first, second),
        check_vma=False,
    )
```

```python
import functools
import math

import jax
import jax.numpy as jnp
from jax import lax
from jax.experimental import pallas as pl
from jax.experimental.pallas import tpu as pltpu
from jax.sharding import PartitionSpec as P

BF = jnp.bfloat16
F32 = jnp.float32
CAP = 20
GROUPS = ((1, 3), (2, 0))
META = 16
LANES = 128
HBM = pl.BlockSpec(memory_space=pltpu.HBM)
SMALL, LARGE = 12, 60
MIB = 1024 * 1024


def mm(a, b, dims):
    return lax.dot_general(a, b, (dims, ((), ())), preferred_element_type=F32)


def ones(mask):
    return jnp.where(mask, 1.0, 0.0).astype(BF)


def eights(count):
    return -(-count // 8) * 8


NN = ((1,), (0,))
NT = ((1,), (1,))
TN = ((0,), (0,))


def positions(names, experts):
    tokens = names.shape[1]
    expert = lax.broadcasted_iota(jnp.int32, (experts, tokens), 0).astype(F32)
    member = (names[0:1] == expert) | (names[1:2] == expert)
    first = lax.broadcasted_iota(jnp.int32, (tokens, tokens), 0)
    second = lax.broadcasted_iota(jnp.int32, (tokens, tokens), 1)
    earlier = jnp.where(first < second, 1.0, 0.0).astype(BF)
    count = mm(jnp.where(member, 1.0, 0.0).astype(BF), earlier, NN)
    return jnp.where(member, count, -1.0)


def row_owner(experts, span):
    rows = experts * span
    row = lax.broadcasted_iota(jnp.int32, (rows, experts), 0)
    expert = lax.broadcasted_iota(jnp.int32, (rows, experts), 1)
    own = (row >= expert * span) & (row < (expert + 1) * span)
    number = jnp.sum(jnp.where(own, expert, 0).astype(F32), axis=1, keepdims=True)
    slot = row[:, 0:1].astype(F32) - number * span
    return jnp.where(own, 1.0, 0.0).astype(BF), number, slot


def message_kernel(dy_ref, names_ref, gates_ref, msg_ref):
    tokens, width = dy_ref.shape
    names = names_ref[...].astype(F32)
    gates = gates_ref[...]
    high = gates.astype(BF).astype(F32)
    low = gates - high
    msg_ref[0:tokens, :] = dy_ref[...]
    line = lax.broadcasted_iota(jnp.int32, (META, tokens), 0)
    meta = jnp.zeros((META, tokens), F32)
    for at, part in enumerate((names, high, low)):
        for k in range(2):
            meta = jnp.where(line == 2 * at + k, part[k : k + 1], meta)
    msg_ref[tokens:, :] = jnp.zeros((META, width), BF)
    msg_ref[tokens:, 0:tokens] = meta.astype(BF)


def token_gates(names, gates, experts):
    expert = lax.broadcasted_iota(jnp.int32, (experts, names.shape[1]), 0).astype(F32)
    gate = jnp.where(names[0:1] == expert, gates[0:1], 0.0)
    gate = gate + jnp.where(names[1:2] == expert, gates[1:2], 0.0)
    high = gate.astype(BF)
    return high, (gate - high.astype(F32)).astype(BF)


def pick_kernel(experts, x_ref, names_ref, xs_ref):
    pos = positions(names_ref[...].astype(F32), experts)
    own, _, slot = row_owner(experts, xs_ref.shape[0] // experts)
    picker = mm(own, pos.astype(BF), NN) == slot
    xs_ref[...] = mm(ones(picker), x_ref[...], NN).astype(BF)


def expand_kernel(experts, cap, *refs):
    msgs, out = refs[:-1], refs[-1]
    tokens = msgs[0].shape[0] - META
    dy = jnp.concatenate([m[0:tokens, :] for m in msgs], axis=0)
    here, high, low = [], [], []
    for k, m in enumerate(msgs):
        meta = m[tokens:, 0:tokens].astype(F32)
        p = positions(meta[0:2], experts)
        here.append(jnp.where(p >= 0.0, p + k * cap, -1.0))
        parts = token_gates(meta[0:2], meta[2:4] + meta[4:6], experts)
        high.append(parts[0])
        low.append(parts[1])
    here, high, low = (jnp.concatenate(v, axis=1) for v in (here, high, low))
    own, _, slot = row_owner(experts, out.shape[0] // experts)
    picker = mm(own, here.astype(BF), NN) == slot
    gate = jnp.where(picker, mm(own, high, NN) + mm(own, low, NN), 0.0)
    gate = jnp.sum(gate, axis=1, keepdims=True)
    out[...] = (mm(ones(picker), dy, NN) * gate).astype(BF)


def regroup(experts, span, count):
    _, number, slot = row_owner(experts, span)
    want = jnp.where(slot < count, number * count + slot, -1.0)
    shape = (experts * span, experts * count)
    return ones(lax.broadcasted_iota(jnp.int32, shape, 1).astype(F32) == want)


def gather(experts, count, span, base):
    _, number, slot = row_owner(experts, count)
    want = number * span + (base + slot)
    shape = (experts * count, experts * span)
    return ones(lax.broadcasted_iota(jnp.int32, shape, 1).astype(F32) == want)


def split_kernel(experts, got_ref, out_ref):
    take = gather(experts, out_ref.shape[0] // experts, got_ref.shape[0] // experts, 0)
    out_ref[...] = mm(take, got_ref[...], NN).astype(BF)


def fill(start, parts, target):
    at, started = 0, []
    for part in parts:
        rows = part.shape[0]
        started.append(start(part, target.at[pl.ds(at, rows)]))
        at += rows
    return started


def rows_kernel(experts, parts, blocks, *refs):
    xs, refs = refs[:parts], refs[parts:]
    got_ref, wi_mine, wi_other, wo_mine, wo_other = refs[:5]
    hid_out, dpre_out, dy_out, *dxs = refs[5 : 8 + blocks]
    x_ref, got, dy_ref, wi_ref, wo_ref, hid_ref, dpre_ref, dx_ref, gate_ref, sems = refs[8 + blocks :]
    width = x_ref.shape[1]
    count = x_ref.shape[0]
    block = count // blocks
    units = wi_mine.shape[0]
    message = block + META
    coeff = math.sqrt(2.0 / math.pi)
    copies = []

    def start(source, target):
        copies.append(pltpu.make_async_copy(source, target, sems.at[len(copies)]))
        copies[-1].start()
        return copies[-1]

    mine, other = pl.ds(0, units), pl.ds(units, units)
    loads = [
        lambda: fill(start, xs, x_ref) + [start(wi_mine, wi_ref.at[mine])],
        lambda: [start(got_ref, got), start(wo_mine, wo_ref.at[mine])],
        lambda: [start(wi_other, wi_ref.at[other]), start(wo_other, wo_ref.at[other])],
    ]
    waits = [loads[0]()]

    def arrived(at):
        if at + 1 < len(loads):
            waits.append(loads[at + 1]())
        for c in waits[at]:
            c.wait()

    tiles = [(at, min(256, count - at)) for at in range(0, count, 256)]
    sums = [0.0] * len(tiles)
    last = []
    for half in range(2):
        spot = pl.ds(half * units, units)
        arrived(2 if half else 0)
        pres = [mm(wi_ref[spot, :], x_ref[at : at + size, :], NT) for at, size in tiles]
        if half == 0:
            arrived(1)
            cap = block // experts
            for j in range(blocks):
                take = gather(experts, cap, blocks * cap, j * cap)
                dy_ref[pl.ds(j * block, block), :] = mm(take, got[...], NN).astype(BF)
            last.append(start(dy_ref, dy_out))
        for i, (at, size) in enumerate(tiles):
            pre = pres[i]
            back = mm(wo_ref[spot, :], dy_ref[at : at + size, :], NT)
            square = pre * pre
            tanh = jnp.tanh(coeff * pre * (1.0 + 0.044715 * square))
            gate = 0.5 * (1.0 + tanh)
            hidden = (pre * gate).astype(BF)
            slope = gate + 0.5 * coeff * pre * (1.0 - tanh * tanh) * (1.0 + 3.0 * 0.044715 * square)
            hid_ref[spot, at : at + size] = hidden
            dpre_ref[spot, at : at + size] = (back * slope).astype(BF)
            prod = hidden.astype(F32) * back
            sums[i] = sums[i] + jnp.sum(prod.reshape(units // META, META, size), axis=0)
        last.append(start(hid_ref.at[spot], hid_out.at[spot]))
        last.append(start(dpre_ref.at[spot], dpre_out.at[spot]))
    for (at, size), part in zip(tiles, sums):
        gate_ref[:, at : at + size] = part.astype(BF)
    for j in range(blocks):
        at = j * message
        dx_ref[at + block : at + message, :] = jnp.zeros((META, width), BF)
        dx_ref[at + block : at + message, 0:block] = gate_ref[:, j * block : (j + 1) * block]
    done = 0
    for edge in (-(-block // LANES) * LANES, count):
        dx = mm(dpre_ref[:, done:edge], wi_ref[...], TN).astype(BF)
        for j in range(blocks):
            low, high = max(done, j * block), min(edge, (j + 1) * block)
            if low < high:
                to = low + j * META
                dx_ref[to : to + high - low, :] = dx[low - done : high - done]
                if high == (j + 1) * block:
                    last.append(start(dx_ref.at[pl.ds(j * message, message)], dxs[j]))
        done = edge
    for c in last:
        c.wait()


def spare(experts, span, at, across):
    shape = (experts, experts * span) if across else (experts * span, experts)
    row = lax.broadcasted_iota(jnp.int32, shape, 1 if across else 0)
    expert = lax.broadcasted_iota(jnp.int32, shape, 0 if across else 1)
    return ones(row == expert * span + at)


def add_kernel(experts, cap, *refs):
    out = refs[-1]
    span = out.shape[0] // experts
    block = experts * cap
    total = refs[0][...].astype(F32)
    for r in refs[1:-1]:
        total = total + r[...].astype(F32)
    sums = jnp.sum(total[block:, 0:block], axis=0, keepdims=True)
    lane = lax.broadcasted_iota(jnp.int32, (experts, block), 1)
    expert = lax.broadcasted_iota(jnp.int32, (experts, block), 0)
    sums = jnp.where((lane >= expert * cap) & (lane < (expert + 1) * cap), sums, 0.0)
    high = sums.astype(BF)
    low = (sums - high.astype(F32)).astype(BF)
    _, _, slot = row_owner(experts, cap)
    column = ones(lax.broadcasted_iota(jnp.int32, (block, LANES), 1).astype(F32) == slot)
    laid = mm(regroup(experts, span, cap), total[0:block].astype(BF), NN)
    first = mm(spare(experts, span, cap, False), mm(high, column, NN).astype(BF), NN)
    first = first + mm(spare(experts, span, cap + 1, False), mm(low, column, NN).astype(BF), NN)
    out[...] = laid.astype(BF)
    out[:, 0:LANES] = (laid[:, 0:LANES] + first).astype(BF)


def weights_kernel(groups, parts, *refs):
    ins, xs, refs = refs[: 3 * groups], refs[3 * groups :][:parts], refs[3 * groups + parts :]
    outs, (held_hid, held_dpre, held_dy, held_x), stored, sems = refs[:3], refs[3:7], refs[7:10], refs[10]
    units = stored[0].shape[0]
    copies = []

    def start(source, target):
        copies.append(pltpu.make_async_copy(source, target, sems.at[len(copies)]))
        copies[-1].start()
        return copies[-1]

    def columns(which, target):
        at, started = 0, []
        for part in ins[which::3]:
            count = part.shape[1]
            started.append(start(part, target.at[:, pl.ds(at, count)]))
            at += count
        return started

    waits = [columns(0, held_hid) + fill(start, ins[2::3], held_dy)]
    waits.append(columns(1, held_dpre) + fill(start, xs, held_x))
    last = []
    for which, (left, right) in enumerate(((held_hid, held_dy), (held_dpre, held_x))):
        for w in waits[which]:
            w.wait()
        for half in (1, 0):
            part = mm(left[pl.ds(half * units, units), :], right[...], NN).astype(BF)
            spot = pl.ds(which * units if half else 0, units)
            target = 2 if half else which
            stored[target][spot, :] = part
            last.append(start(stored[target].at[spot], outs[target].at[spot]))
    for c in last:
        c.wait()


def combine_kernel(experts, cap, names_ref, gates_ref, ret_ref, dx_ref, gate_ref):
    names = names_ref[...].astype(F32)
    pos = positions(names, experts)
    span = ret_ref.shape[0] // experts
    own, _, slot = row_owner(experts, span)
    picker = mm(own, pos.astype(BF), NN) == slot
    dx_ref[...] = mm(ones(picker), ret_ref[...], TN).astype(BF)
    table = mm(spare(experts, span, cap, True), ret_ref[:, 0:LANES], NN)
    table = table + mm(spare(experts, span, cap + 1, True), ret_ref[:, 0:LANES], NN)
    value = jnp.zeros(pos.shape, F32)
    for s in range(cap):
        value = jnp.where(pos == float(s), table[:, s : s + 1], value)
    expert = lax.broadcasted_iota(jnp.int32, pos.shape, 0).astype(F32)
    sums = [
        jnp.sum(jnp.where(expert == names[k : k + 1], value, 0.0), axis=0, keepdims=True)
        for k in range(2)
    ]
    line = lax.broadcasted_iota(jnp.int32, gate_ref.shape, 0)
    gate_ref[...] = jnp.where(line == 0, sums[0], sums[1]) / gates_ref[...]


def call(kernel, outs, vmem, **more):
    return pl.pallas_call(
        kernel,
        out_shape=outs,
        compiler_params=pltpu.CompilerParams(vmem_limit_bytes=vmem * MIB),
        cost_estimate=pl.CostEstimate(flops=1, bytes_accessed=1, transcendentals=0),
        **more,
    )


def shift(value, axis, by):
    size = lax.axis_size(axis)
    return lax.ppermute(value, axis, [(i, (i + by) % size) for i in range(size)])


def exchange(value):
    return lax.all_to_all(value, "expert", split_axis=0, concat_axis=0, tiled=True)


def local(hidden_in, grad_out, combine, routes, w_in, w_out):
    tokens, width = hidden_in.shape
    units = w_out.shape[1]
    experts = lax.axis_size("expert")
    planes = lax.axis_size("dp")
    names, gates = routes.T, combine.T
    wi, wo = w_in[0].T, w_out[0]
    hidden_units = 2 * units
    block = experts * CAP
    after = lax.optimization_barrier

    def arr(*shape, kind=BF):
        return jax.ShapeDtypeStruct(shape, kind)

    msg = call(message_kernel, arr(tokens + META, width), SMALL)(grad_out, names, gates)
    msgs = {0: msg}
    for k in (1, 3, 2):
        msgs[k] = shift(msg, "dp", k)
    xs = call(functools.partial(pick_kernel, experts), arr(experts * eights(CAP), width), LARGE)(
        hidden_in, names
    )
    wi_other, wo_other = shift(wi, "seq", 1), shift(wo, "seq", 1)
    msgs[1], wi_other, wo_other = after((msgs[1], wi_other, wo_other))
    xa, msgs[1], msgs[3] = after((exchange(xs), msgs[1], msgs[3]))
    x = call(functools.partial(split_kernel, experts), arr(block, width), SMALL)(xa)
    x, msgs[1] = after((x, msgs[1]))
    near = [shift(x, "dp", 1), shift(x, "dp", -1)]
    def expand(g):
        return call(
            functools.partial(expand_kernel, experts, CAP),
            arr(block * len(GROUPS[g]), width),
            SMALL,
        )(*(msgs[k] for k in GROUPS[g]))

    sent, msgs[2] = after((expand(0), msgs[2]))
    got = exchange(sent)
    sent, got, near = after((expand(1), got, near))
    got = [got, exchange(sent)]
    far, near = after((x, near))
    xs = {0: [x], 1: near[:1], 2: [shift(far, "dp", 2)], 3: near[1:]}

    def rows_call(g):
        blocks = len(GROUPS[g])
        count = blocks * block
        parts = sum((xs[k] for k in GROUPS[g]), [])
        hid, dpre, dy, *dx = call(
            functools.partial(rows_kernel, experts, len(parts), blocks),
            [arr(hidden_units, count)] * 2
            + [arr(count, width)]
            + [arr(block + META, width)] * blocks,
            LARGE,
            in_specs=[HBM] * (len(parts) + 5),
            out_specs=[HBM] * (3 + blocks),
            scratch_shapes=[pltpu.VMEM((count, width), BF)] * 3
            + [pltpu.VMEM((hidden_units, width), BF)] * 2
            + [pltpu.VMEM((hidden_units, count), BF)] * 2
            + [pltpu.VMEM((count + META * blocks, width), BF), pltpu.VMEM((META, count), BF)]
            + [pltpu.SemaphoreType.DMA((32,))],
        )(*parts, got[g], wi, wi_other, wo, wo_other)
        return [hid, dpre, dy], parts, dict(zip(GROUPS[g], dx))

    done_a, parts_a, dx = rows_call(0)
    dx = {k: shift(v, "dp", -k) for k, v in dx.items()}
    done_b, parts_b, dx_b = rows_call(1)
    dx[0], dx[2] = dx_b[0], shift(dx_b[2], "dp", 2)
    grads = [(units, width)] * 2 + [(2 * units, width)]
    total = planes * block
    ins = done_a + done_b + parts_a + parts_b
    mine_o, mine_i, theirs = call(
        functools.partial(weights_kernel, len(GROUPS), len(parts_a + parts_b)),
        [arr(*g) for g in grads],
        LARGE,
        in_specs=[HBM] * len(ins),
        out_specs=[HBM] * 3,
        scratch_shapes=[pltpu.VMEM((hidden_units, total), BF)] * 2
        + [pltpu.VMEM((total, width), BF)] * 2
        + [pltpu.VMEM(g, BF) for g in grads]
        + [pltpu.SemaphoreType.DMA((32,))],
    )(*ins)
    dx, theirs = after((dx, theirs))
    back = call(
        functools.partial(add_kernel, experts, CAP), arr(experts * eights(CAP), width), SMALL
    )(*(dx[k] for k in range(planes)))
    theirs, back = after((theirs, back))
    theirs = shift(theirs, "seq", 1).astype(F32)
    grad_wo = (mine_o.astype(F32) + theirs[:units]).astype(BF)
    grad_wi = (mine_i.astype(F32) + theirs[units:]).astype(BF)
    back, grad_wo, grad_wi = after((exchange(back), grad_wo, grad_wi))
    grad_x, grad_gate = call(
        functools.partial(combine_kernel, experts, CAP),
        [arr(tokens, width), arr(2, tokens, kind=F32)],
        SMALL,
    )(names, gates, back)
    return grad_x, grad_gate.T, grad_wi.T[None], grad_wo[None]


def solution(mesh):
    rows = P(("dp", "seq", "expert"), None)
    first = P("expert", None, ("dp", "seq"))
    second = P("expert", ("dp", "seq"), None)
    return jax.shard_map(
        local,
        mesh=mesh,
        in_specs=(rows, rows, rows, rows, first, second),
        out_specs=(rows, rows, first, second),
        check_vma=False,
    )
```

```python
import functools
import math

import jax
import jax.numpy as jnp
from jax import lax
from jax.experimental import pallas as pl
from jax.experimental.pallas import tpu as pltpu
from jax.sharding import PartitionSpec as P

BF = jnp.bfloat16
F32 = jnp.float32
CAP = 20
GROUPS = ((1, 3), (2, 0))
META = 16
LANES = 128
HBM = pl.BlockSpec(memory_space=pltpu.HBM)
SMALL, LARGE = 12, 60
MIB = 1024 * 1024


def mm(a, b, dims):
    return lax.dot_general(a, b, (dims, ((), ())), preferred_element_type=F32)


def ones(mask):
    return jnp.where(mask, 1.0, 0.0).astype(BF)


def eights(count):
    return -(-count // 8) * 8


NN = ((1,), (0,))
NT = ((1,), (1,))
TN = ((0,), (0,))


def positions(names, experts):
    tokens = names.shape[1]
    expert = lax.broadcasted_iota(jnp.int32, (experts, tokens), 0).astype(F32)
    member = (names[0:1] == expert) | (names[1:2] == expert)
    first = lax.broadcasted_iota(jnp.int32, (tokens, tokens), 0)
    second = lax.broadcasted_iota(jnp.int32, (tokens, tokens), 1)
    earlier = jnp.where(first < second, 1.0, 0.0).astype(BF)
    count = mm(jnp.where(member, 1.0, 0.0).astype(BF), earlier, NN)
    return jnp.where(member, count, -1.0)


def row_owner(experts, span):
    rows = experts * span
    row = lax.broadcasted_iota(jnp.int32, (rows, experts), 0)
    expert = lax.broadcasted_iota(jnp.int32, (rows, experts), 1)
    own = (row >= expert * span) & (row < (expert + 1) * span)
    number = jnp.sum(jnp.where(own, expert, 0).astype(F32), axis=1, keepdims=True)
    slot = row[:, 0:1].astype(F32) - number * span
    return jnp.where(own, 1.0, 0.0).astype(BF), number, slot


def message_kernel(dy_ref, names_ref, gates_ref, msg_ref):
    tokens, width = dy_ref.shape
    names = names_ref[...].astype(F32)
    gates = gates_ref[...]
    high = gates.astype(BF).astype(F32)
    low = gates - high
    msg_ref[0:tokens, :] = dy_ref[...]
    line = lax.broadcasted_iota(jnp.int32, (META, tokens), 0)
    meta = jnp.zeros((META, tokens), F32)
    for at, part in enumerate((names, high, low)):
        for k in range(2):
            meta = jnp.where(line == 2 * at + k, part[k : k + 1], meta)
    msg_ref[tokens:, :] = jnp.zeros((META, width), BF)
    msg_ref[tokens:, 0:tokens] = meta.astype(BF)


def token_gates(names, gates, experts):
    expert = lax.broadcasted_iota(jnp.int32, (experts, names.shape[1]), 0).astype(F32)
    gate = jnp.where(names[0:1] == expert, gates[0:1], 0.0)
    gate = gate + jnp.where(names[1:2] == expert, gates[1:2], 0.0)
    high = gate.astype(BF)
    return high, (gate - high.astype(F32)).astype(BF)


def pick_kernel(experts, x_ref, names_ref, xs_ref):
    pos = positions(names_ref[...].astype(F32), experts)
    own, _, slot = row_owner(experts, xs_ref.shape[0] // experts)
    picker = mm(own, pos.astype(BF), NN) == slot
    xs_ref[...] = mm(ones(picker), x_ref[...], NN).astype(BF)


def expand_kernel(experts, cap, *refs):
    msgs, out = refs[:-1], refs[-1]
    tokens = msgs[0].shape[0] - META
    dy = jnp.concatenate([m[0:tokens, :] for m in msgs], axis=0)
    here, high, low = [], [], []
    for k, m in enumerate(msgs):
        meta = m[tokens:, 0:tokens].astype(F32)
        p = positions(meta[0:2], experts)
        here.append(jnp.where(p >= 0.0, p + k * cap, -1.0))
        parts = token_gates(meta[0:2], meta[2:4] + meta[4:6], experts)
        high.append(parts[0])
        low.append(parts[1])
    here, high, low = (jnp.concatenate(v, axis=1) for v in (here, high, low))
    own, _, slot = row_owner(experts, out.shape[0] // experts)
    picker = mm(own, here.astype(BF), NN) == slot
    gate = jnp.where(picker, mm(own, high, NN) + mm(own, low, NN), 0.0)
    gate = jnp.sum(gate, axis=1, keepdims=True)
    out[...] = (mm(ones(picker), dy, NN) * gate).astype(BF)


def regroup(experts, span, count):
    _, number, slot = row_owner(experts, span)
    want = jnp.where(slot < count, number * count + slot, -1.0)
    shape = (experts * span, experts * count)
    return ones(lax.broadcasted_iota(jnp.int32, shape, 1).astype(F32) == want)


def gather(experts, count, span, base):
    _, number, slot = row_owner(experts, count)
    want = number * span + (base + slot)
    shape = (experts * count, experts * span)
    return ones(lax.broadcasted_iota(jnp.int32, shape, 1).astype(F32) == want)


def split_kernel(experts, got_ref, out_ref):
    take = gather(experts, out_ref.shape[0] // experts, got_ref.shape[0] // experts, 0)
    out_ref[...] = mm(take, got_ref[...], NN).astype(BF)


def fill(start, parts, target):
    at, started = 0, []
    for part in parts:
        rows = part.shape[0]
        started.append(start(part, target.at[pl.ds(at, rows)]))
        at += rows
    return started


def rows_kernel(experts, parts, blocks, *refs):
    xs, refs = refs[:parts], refs[parts:]
    got_ref, wi_mine, wi_other, wo_mine, wo_other = refs[:5]
    hid_out, dpre_out, dy_out, *dxs = refs[5 : 8 + blocks]
    x_ref, got, dy_ref, wi_ref, wo_ref, hid_ref, dpre_ref, dx_ref, gate_ref, sems = refs[8 + blocks :]
    width = x_ref.shape[1]
    count = x_ref.shape[0]
    block = count // blocks
    units = wi_mine.shape[0]
    message = block + META
    coeff = math.sqrt(2.0 / math.pi)
    copies = []

    def start(source, target):
        copies.append(pltpu.make_async_copy(source, target, sems.at[len(copies)]))
        copies[-1].start()
        return copies[-1]

    mine, other = pl.ds(0, units), pl.ds(units, units)
    loads = [
        lambda: fill(start, xs, x_ref) + [start(wi_mine, wi_ref.at[mine])],
        lambda: [start(got_ref, got), start(wo_mine, wo_ref.at[mine])],
        lambda: [start(wi_other, wi_ref.at[other]), start(wo_other, wo_ref.at[other])],
    ]
    waits = [loads[0]()]

    def arrived(at):
        if at + 1 < len(loads):
            waits.append(loads[at + 1]())
        for c in waits[at]:
            c.wait()

    tiles = [(at, min(256, count - at)) for at in range(0, count, 256)]
    sums = [0.0] * len(tiles)
    last = []
    for half in range(2):
        spot = pl.ds(half * units, units)
        arrived(2 if half else 0)
        pres = [mm(wi_ref[spot, :], x_ref[at : at + size, :], NT) for at, size in tiles]
        if half == 0:
            arrived(1)
            cap = block // experts
            for j in range(blocks):
                take = gather(experts, cap, blocks * cap, j * cap)
                dy_ref[pl.ds(j * block, block), :] = mm(take, got[...], NN).astype(BF)
            last.append(start(dy_ref, dy_out))
        for i, (at, size) in enumerate(tiles):
            pre = pres[i]
            back = mm(wo_ref[spot, :], dy_ref[at : at + size, :], NT)
            square = pre * pre
            tanh = jnp.tanh(coeff * pre * (1.0 + 0.044715 * square))
            gate = 0.5 * (1.0 + tanh)
            hidden = (pre * gate).astype(BF)
            slope = gate + 0.5 * coeff * pre * (1.0 - tanh * tanh) * (1.0 + 3.0 * 0.044715 * square)
            hid_ref[spot, at : at + size] = hidden
            dpre_ref[spot, at : at + size] = (back * slope).astype(BF)
            prod = hidden.astype(F32) * back
            sums[i] = sums[i] + jnp.sum(prod.reshape(units // META, META, size), axis=0)
        last.append(start(hid_ref.at[spot], hid_out.at[spot]))
        last.append(start(dpre_ref.at[spot], dpre_out.at[spot]))
    for (at, size), part in zip(tiles, sums):
        gate_ref[:, at : at + size] = part.astype(BF)
    for j in range(blocks):
        at = j * message
        dx_ref[at + block : at + message, :] = jnp.zeros((META, width), BF)
        dx_ref[at + block : at + message, 0:block] = gate_ref[:, j * block : (j + 1) * block]
    done = 0
    for edge in (-(-block // LANES) * LANES, count):
        dx = mm(dpre_ref[:, done:edge], wi_ref[...], TN).astype(BF)
        for j in range(blocks):
            low, high = max(done, j * block), min(edge, (j + 1) * block)
            if low < high:
                to = low + j * META
                dx_ref[to : to + high - low, :] = dx[low - done : high - done]
                if high == (j + 1) * block:
                    last.append(start(dx_ref.at[pl.ds(j * message, message)], dxs[j]))
        done = edge
    for c in last:
        c.wait()


def spare(experts, span, at, across):
    shape = (experts, experts * span) if across else (experts * span, experts)
    row = lax.broadcasted_iota(jnp.int32, shape, 1 if across else 0)
    expert = lax.broadcasted_iota(jnp.int32, shape, 0 if across else 1)
    return ones(row == expert * span + at)


def add_kernel(experts, cap, *refs):
    out = refs[-1]
    span = out.shape[0] // experts
    block = experts * cap
    total = refs[0][...].astype(F32)
    for r in refs[1:-1]:
        total = total + r[...].astype(F32)
    sums = jnp.sum(total[block:, 0:block], axis=0, keepdims=True)
    lane = lax.broadcasted_iota(jnp.int32, (experts, block), 1)
    expert = lax.broadcasted_iota(jnp.int32, (experts, block), 0)
    sums = jnp.where((lane >= expert * cap) & (lane < (expert + 1) * cap), sums, 0.0)
    high = sums.astype(BF)
    low = (sums - high.astype(F32)).astype(BF)
    _, _, slot = row_owner(experts, cap)
    column = ones(lax.broadcasted_iota(jnp.int32, (block, LANES), 1).astype(F32) == slot)
    laid = mm(regroup(experts, span, cap), total[0:block].astype(BF), NN)
    first = mm(spare(experts, span, cap, False), mm(high, column, NN).astype(BF), NN)
    first = first + mm(spare(experts, span, cap + 1, False), mm(low, column, NN).astype(BF), NN)
    out[...] = laid.astype(BF)
    out[:, 0:LANES] = (laid[:, 0:LANES] + first).astype(BF)


def weights_kernel(groups, parts, *refs):
    ins, xs, refs = refs[: 3 * groups], refs[3 * groups :][:parts], refs[3 * groups + parts :]
    outs, (held_hid, held_dpre, held_dy, held_x), stored, sems = refs[:3], refs[3:7], refs[7:10], refs[10]
    units = stored[0].shape[0]
    copies = []

    def start(source, target):
        copies.append(pltpu.make_async_copy(source, target, sems.at[len(copies)]))
        copies[-1].start()
        return copies[-1]

    def columns(which, target):
        at, started = 0, []
        for part in ins[which::3]:
            count = part.shape[1]
            started.append(start(part, target.at[:, pl.ds(at, count)]))
            at += count
        return started

    waits = [columns(0, held_hid) + fill(start, ins[2::3], held_dy)]
    waits.append(columns(1, held_dpre) + fill(start, xs, held_x))
    last = []
    for which, (left, right) in enumerate(((held_hid, held_dy), (held_dpre, held_x))):
        for w in waits[which]:
            w.wait()
        for half in (1, 0):
            part = mm(left[pl.ds(half * units, units), :], right[...], NN).astype(BF)
            spot = pl.ds(which * units if half else 0, units)
            target = 2 if half else which
            stored[target][spot, :] = part
            last.append(start(stored[target].at[spot], outs[target].at[spot]))
    for c in last:
        c.wait()


def combine_kernel(experts, cap, names_ref, gates_ref, ret_ref, dx_ref, gate_ref):
    names = names_ref[...].astype(F32)
    pos = positions(names, experts)
    span = ret_ref.shape[0] // experts
    own, _, slot = row_owner(experts, span)
    picker = mm(own, pos.astype(BF), NN) == slot
    dx_ref[...] = mm(ones(picker), ret_ref[...], TN).astype(BF)
    table = mm(spare(experts, span, cap, True), ret_ref[:, 0:LANES], NN)
    table = table + mm(spare(experts, span, cap + 1, True), ret_ref[:, 0:LANES], NN)
    value = jnp.zeros(pos.shape, F32)
    for s in range(cap):
        value = jnp.where(pos == float(s), table[:, s : s + 1], value)
    expert = lax.broadcasted_iota(jnp.int32, pos.shape, 0).astype(F32)
    sums = [
        jnp.sum(jnp.where(expert == names[k : k + 1], value, 0.0), axis=0, keepdims=True)
        for k in range(2)
    ]
    line = lax.broadcasted_iota(jnp.int32, gate_ref.shape, 0)
    gate_ref[...] = jnp.where(line == 0, sums[0], sums[1]) / gates_ref[...]


def call(kernel, outs, vmem, **more):
    return pl.pallas_call(
        kernel,
        out_shape=outs,
        compiler_params=pltpu.CompilerParams(vmem_limit_bytes=vmem * MIB),
        cost_estimate=pl.CostEstimate(flops=1, bytes_accessed=1, transcendentals=0),
        **more,
    )


def shift(value, axis, by):
    size = lax.axis_size(axis)
    return lax.ppermute(value, axis, [(i, (i + by) % size) for i in range(size)])


def exchange(value):
    return lax.all_to_all(value, "expert", split_axis=0, concat_axis=0, tiled=True)


def local(hidden_in, grad_out, combine, routes, w_in, w_out):
    tokens, width = hidden_in.shape
    units = w_out.shape[1]
    experts = lax.axis_size("expert")
    planes = lax.axis_size("dp")
    names, gates = routes.T, combine.T
    wi, wo = w_in[0].T, w_out[0]
    hidden_units = 2 * units
    block = experts * CAP
    after = lax.optimization_barrier

    def arr(*shape, kind=BF):
        return jax.ShapeDtypeStruct(shape, kind)

    msg = call(message_kernel, arr(tokens + META, width), SMALL)(grad_out, names, gates)
    msgs = {0: msg}
    for k in (1, 3, 2):
        msgs[k] = shift(msg, "dp", k)
    xs = call(functools.partial(pick_kernel, experts), arr(experts * eights(CAP), width), LARGE)(
        hidden_in, names
    )
    wi, wo, _ = after((wi, wo, xs))
    wi_other, wo_other = shift(wi, "seq", 1), shift(wo, "seq", 1)
    msgs[1], wi_other, wo_other = after((msgs[1], wi_other, wo_other))
    xa, msgs[1], msgs[3] = after((exchange(xs), msgs[1], msgs[3]))
    x = call(functools.partial(split_kernel, experts), arr(block, width), SMALL)(xa)
    x, msgs[1] = after((x, msgs[1]))
    near = [shift(x, "dp", 1), shift(x, "dp", -1)]
    def expand(g):
        return call(
            functools.partial(expand_kernel, experts, CAP),
            arr(block * len(GROUPS[g]), width),
            SMALL,
        )(*(msgs[k] for k in GROUPS[g]))

    sent, msgs[2] = after((expand(0), msgs[2]))
    got = exchange(sent)
    sent, got, near = after((expand(1), got, near))
    got = [got, exchange(sent)]
    far, near = after((x, near))
    xs = {0: [x], 1: near[:1], 2: [shift(far, "dp", 2)], 3: near[1:]}

    def rows_call(g):
        blocks = len(GROUPS[g])
        count = blocks * block
        parts = sum((xs[k] for k in GROUPS[g]), [])
        hid, dpre, dy, *dx = call(
            functools.partial(rows_kernel, experts, len(parts), blocks),
            [arr(hidden_units, count)] * 2
            + [arr(count, width)]
            + [arr(block + META, width)] * blocks,
            LARGE,
            in_specs=[HBM] * (len(parts) + 5),
            out_specs=[HBM] * (3 + blocks),
            scratch_shapes=[pltpu.VMEM((count, width), BF)] * 3
            + [pltpu.VMEM((hidden_units, width), BF)] * 2
            + [pltpu.VMEM((hidden_units, count), BF)] * 2
            + [pltpu.VMEM((count + META * blocks, width), BF), pltpu.VMEM((META, count), BF)]
            + [pltpu.SemaphoreType.DMA((32,))],
        )(*parts, got[g], wi, wi_other, wo, wo_other)
        return [hid, dpre, dy], parts, dict(zip(GROUPS[g], dx))

    done_a, parts_a, dx = rows_call(0)
    dx = {k: shift(v, "dp", -k) for k, v in dx.items()}
    done_b, parts_b, dx_b = rows_call(1)
    dx[0], dx[2] = dx_b[0], shift(dx_b[2], "dp", 2)
    grads = [(units, width)] * 2 + [(2 * units, width)]
    total = planes * block
    ins = done_a + done_b + parts_a + parts_b
    mine_o, mine_i, theirs = call(
        functools.partial(weights_kernel, len(GROUPS), len(parts_a + parts_b)),
        [arr(*g) for g in grads],
        LARGE,
        in_specs=[HBM] * len(ins),
        out_specs=[HBM] * 3,
        scratch_shapes=[pltpu.VMEM((hidden_units, total), BF)] * 2
        + [pltpu.VMEM((total, width), BF)] * 2
        + [pltpu.VMEM(g, BF) for g in grads]
        + [pltpu.SemaphoreType.DMA((32,))],
    )(*ins)
    dx, theirs = after((dx, theirs))
    back = call(
        functools.partial(add_kernel, experts, CAP), arr(experts * eights(CAP), width), SMALL
    )(*(dx[k] for k in range(planes)))
    theirs, back = after((theirs, back))
    theirs = shift(theirs, "seq", 1).astype(F32)
    grad_wo = (mine_o.astype(F32) + theirs[:units]).astype(BF)
    grad_wi = (mine_i.astype(F32) + theirs[units:]).astype(BF)
    back, grad_wo, grad_wi = after((exchange(back), grad_wo, grad_wi))
    grad_x, grad_gate = call(
        functools.partial(combine_kernel, experts, CAP),
        [arr(tokens, width), arr(2, tokens, kind=F32)],
        SMALL,
    )(names, gates, back)
    return grad_x, grad_gate.T, grad_wi.T[None], grad_wo[None]


def solution(mesh):
    rows = P(("dp", "seq", "expert"), None)
    first = P("expert", None, ("dp", "seq"))
    second = P("expert", ("dp", "seq"), None)
    return jax.shard_map(
        local,
        mesh=mesh,
        in_specs=(rows, rows, rows, rows, first, second),
        out_specs=(rows, rows, first, second),
        check_vma=False,
    )
```

```python
import functools
import math

import jax
import jax.numpy as jnp
from jax import lax
from jax.experimental import pallas as pl
from jax.experimental.pallas import tpu as pltpu
from jax.sharding import PartitionSpec as P

BF = jnp.bfloat16
F32 = jnp.float32
CAP = 20
GROUPS = ((1, 3), (2, 0))
META = 16
LANES = 128
HBM = pl.BlockSpec(memory_space=pltpu.HBM)
SMALL, LARGE = 12, 60
MIB = 1024 * 1024


def mm(a, b, dims):
    return lax.dot_general(a, b, (dims, ((), ())), preferred_element_type=F32)


def ones(mask):
    return jnp.where(mask, 1.0, 0.0).astype(BF)


def eights(count):
    return -(-count // 8) * 8


NN = ((1,), (0,))
NT = ((1,), (1,))
TN = ((0,), (0,))


def positions(names, experts):
    tokens = names.shape[1]
    expert = lax.broadcasted_iota(jnp.int32, (experts, tokens), 0).astype(F32)
    member = (names[0:1] == expert) | (names[1:2] == expert)
    first = lax.broadcasted_iota(jnp.int32, (tokens, tokens), 0)
    second = lax.broadcasted_iota(jnp.int32, (tokens, tokens), 1)
    earlier = jnp.where(first < second, 1.0, 0.0).astype(BF)
    count = mm(jnp.where(member, 1.0, 0.0).astype(BF), earlier, NN)
    return jnp.where(member, count, -1.0)


def row_owner(experts, span):
    rows = experts * span
    row = lax.broadcasted_iota(jnp.int32, (rows, experts), 0)
    expert = lax.broadcasted_iota(jnp.int32, (rows, experts), 1)
    own = (row >= expert * span) & (row < (expert + 1) * span)
    number = jnp.sum(jnp.where(own, expert, 0).astype(F32), axis=1, keepdims=True)
    slot = row[:, 0:1].astype(F32) - number * span
    return jnp.where(own, 1.0, 0.0).astype(BF), number, slot


def message_kernel(dy_ref, names_ref, gates_ref, msg_ref):
    tokens, width = dy_ref.shape
    names = names_ref[...].astype(F32)
    gates = gates_ref[...]
    high = gates.astype(BF).astype(F32)
    low = gates - high
    msg_ref[0:tokens, :] = dy_ref[...]
    line = lax.broadcasted_iota(jnp.int32, (META, tokens), 0)
    meta = jnp.zeros((META, tokens), F32)
    for at, part in enumerate((names, high, low)):
        for k in range(2):
            meta = jnp.where(line == 2 * at + k, part[k : k + 1], meta)
    msg_ref[tokens:, :] = jnp.zeros((META, width), BF)
    msg_ref[tokens:, 0:tokens] = meta.astype(BF)


def token_gates(names, gates, experts):
    expert = lax.broadcasted_iota(jnp.int32, (experts, names.shape[1]), 0).astype(F32)
    gate = jnp.where(names[0:1] == expert, gates[0:1], 0.0)
    gate = gate + jnp.where(names[1:2] == expert, gates[1:2], 0.0)
    high = gate.astype(BF)
    return high, (gate - high.astype(F32)).astype(BF)


def pick_kernel(experts, x_ref, names_ref, xs_ref):
    pos = positions(names_ref[...].astype(F32), experts)
    own, _, slot = row_owner(experts, xs_ref.shape[0] // experts)
    picker = mm(own, pos.astype(BF), NN) == slot
    xs_ref[...] = mm(ones(picker), x_ref[...], NN).astype(BF)


def expand_kernel(experts, cap, *refs):
    msgs, out = refs[:-1], refs[-1]
    tokens = msgs[0].shape[0] - META
    dy = jnp.concatenate([m[0:tokens, :] for m in msgs], axis=0)
    here, high, low = [], [], []
    for k, m in enumerate(msgs):
        meta = m[tokens:, 0:tokens].astype(F32)
        p = positions(meta[0:2], experts)
        here.append(jnp.where(p >= 0.0, p + k * cap, -1.0))
        parts = token_gates(meta[0:2], meta[2:4] + meta[4:6], experts)
        high.append(parts[0])
        low.append(parts[1])
    here, high, low = (jnp.concatenate(v, axis=1) for v in (here, high, low))
    own, _, slot = row_owner(experts, out.shape[0] // experts)
    picker = mm(own, here.astype(BF), NN) == slot
    picker = ones(picker)
    gate = (mm(picker, high, NT) + mm(picker, low, NT)) * own.astype(F32)
    gate = jnp.sum(gate, axis=1, keepdims=True)
    out[...] = (mm(picker, dy, NN) * gate).astype(BF)


def regroup(experts, span, count):
    _, number, slot = row_owner(experts, span)
    want = jnp.where(slot < count, number * count + slot, -1.0)
    shape = (experts * span, experts * count)
    return ones(lax.broadcasted_iota(jnp.int32, shape, 1).astype(F32) == want)


def gather(experts, count, span, base):
    _, number, slot = row_owner(experts, count)
    want = number * span + (base + slot)
    shape = (experts * count, experts * span)
    return ones(lax.broadcasted_iota(jnp.int32, shape, 1).astype(F32) == want)


def split_kernel(experts, got_ref, out_ref):
    take = gather(experts, out_ref.shape[0] // experts, got_ref.shape[0] // experts, 0)
    out_ref[...] = mm(take, got_ref[...], NN).astype(BF)


def fill(start, parts, target):
    at, started = 0, []
    for part in parts:
        rows = part.shape[0]
        started.append(start(part, target.at[pl.ds(at, rows)]))
        at += rows
    return started


def rows_kernel(experts, parts, blocks, *refs):
    xs, refs = refs[:parts], refs[parts:]
    got_ref, wi_mine, wi_other, wo_mine, wo_other = refs[:5]
    hid_out, dpre_out, dy_out, *dxs = refs[5 : 8 + blocks]
    x_ref, got, dy_ref, wi_ref, wo_ref, hid_ref, dpre_ref, dx_ref, gate_ref, sems = refs[8 + blocks :]
    width = x_ref.shape[1]
    count = x_ref.shape[0]
    block = count // blocks
    units = wi_mine.shape[0]
    message = block + META
    coeff = math.sqrt(2.0 / math.pi)
    copies = []

    def start(source, target):
        copies.append(pltpu.make_async_copy(source, target, sems.at[len(copies)]))
        copies[-1].start()
        return copies[-1]

    mine, other = pl.ds(0, units), pl.ds(units, units)
    loads = [
        lambda: fill(start, xs, x_ref) + [start(wi_mine, wi_ref.at[mine])],
        lambda: [start(got_ref, got), start(wo_mine, wo_ref.at[mine])],
        lambda: [start(wi_other, wi_ref.at[other]), start(wo_other, wo_ref.at[other])],
    ]
    waits = [loads[0]()]

    def arrived(at):
        if at + 1 < len(loads):
            waits.append(loads[at + 1]())
        for c in waits[at]:
            c.wait()

    tiles = [(at, min(256, count - at)) for at in range(0, count, 256)]
    sums = [0.0] * len(tiles)
    last = []
    for half in range(2):
        spot = pl.ds(half * units, units)
        arrived(2 if half else 0)
        pres = [mm(wi_ref[spot, :], x_ref[at : at + size, :], NT) for at, size in tiles]
        if half == 0:
            arrived(1)
            cap = block // experts
            for j in range(blocks):
                take = gather(experts, cap, blocks * cap, j * cap)
                dy_ref[pl.ds(j * block, block), :] = mm(take, got[...], NN).astype(BF)
            last.append(start(dy_ref, dy_out))
        for i, (at, size) in enumerate(tiles):
            pre = pres[i]
            back = mm(wo_ref[spot, :], dy_ref[at : at + size, :], NT)
            square = pre * pre
            tanh = jnp.tanh(coeff * pre * (1.0 + 0.044715 * square))
            gate = 0.5 * (1.0 + tanh)
            hidden = (pre * gate).astype(BF)
            slope = gate + 0.5 * coeff * pre * (1.0 - tanh * tanh) * (1.0 + 3.0 * 0.044715 * square)
            hid_ref[spot, at : at + size] = hidden
            dpre_ref[spot, at : at + size] = (back * slope).astype(BF)
            prod = hidden.astype(F32) * back
            sums[i] = sums[i] + jnp.sum(prod.reshape(units // META, META, size), axis=0)
        last.append(start(hid_ref.at[spot], hid_out.at[spot]))
        last.append(start(dpre_ref.at[spot], dpre_out.at[spot]))
    for (at, size), part in zip(tiles, sums):
        gate_ref[:, at : at + size] = part.astype(BF)
    for j in range(blocks):
        at = j * message
        dx_ref[at + block : at + message, :] = jnp.zeros((META, width), BF)
        dx_ref[at + block : at + message, 0:block] = gate_ref[:, j * block : (j + 1) * block]
    done = 0
    for edge in (-(-block // LANES) * LANES, count):
        dx = mm(dpre_ref[:, done:edge], wi_ref[...], TN).astype(BF)
        for j in range(blocks):
            low, high = max(done, j * block), min(edge, (j + 1) * block)
            if low < high:
                to = low + j * META
                dx_ref[to : to + high - low, :] = dx[low - done : high - done]
                if high == (j + 1) * block:
                    last.append(start(dx_ref.at[pl.ds(j * message, message)], dxs[j]))
        done = edge
    for c in last:
        c.wait()


def spare(experts, span, at, across):
    shape = (experts, experts * span) if across else (experts * span, experts)
    row = lax.broadcasted_iota(jnp.int32, shape, 1 if across else 0)
    expert = lax.broadcasted_iota(jnp.int32, shape, 0 if across else 1)
    return ones(row == expert * span + at)


def add_kernel(experts, cap, *refs):
    out = refs[-1]
    span = out.shape[0] // experts
    block = experts * cap
    total = refs[0][...].astype(F32)
    for r in refs[1:-1]:
        total = total + r[...].astype(F32)
    sums = jnp.sum(total[block:, 0:block], axis=0, keepdims=True)
    lane = lax.broadcasted_iota(jnp.int32, (experts, block), 1)
    expert = lax.broadcasted_iota(jnp.int32, (experts, block), 0)
    sums = jnp.where((lane >= expert * cap) & (lane < (expert + 1) * cap), sums, 0.0)
    high = sums.astype(BF)
    low = (sums - high.astype(F32)).astype(BF)
    _, _, slot = row_owner(experts, cap)
    column = ones(lax.broadcasted_iota(jnp.int32, (block, LANES), 1).astype(F32) == slot)
    laid = mm(regroup(experts, span, cap), total[0:block].astype(BF), NN)
    first = mm(spare(experts, span, cap, False), mm(high, column, NN).astype(BF), NN)
    first = first + mm(spare(experts, span, cap + 1, False), mm(low, column, NN).astype(BF), NN)
    out[...] = laid.astype(BF)
    out[:, 0:LANES] = (laid[:, 0:LANES] + first).astype(BF)


def weights_kernel(groups, parts, *refs):
    ins, xs, refs = refs[: 3 * groups], refs[3 * groups :][:parts], refs[3 * groups + parts :]
    outs, (held_hid, held_dpre, held_dy, held_x), stored, sems = refs[:3], refs[3:7], refs[7:10], refs[10]
    units = stored[0].shape[0]
    copies = []

    def start(source, target):
        copies.append(pltpu.make_async_copy(source, target, sems.at[len(copies)]))
        copies[-1].start()
        return copies[-1]

    def columns(which, target):
        at, started = 0, []
        for part in ins[which::3]:
            count = part.shape[1]
            started.append(start(part, target.at[:, pl.ds(at, count)]))
            at += count
        return started

    waits = [columns(0, held_hid) + fill(start, ins[2::3], held_dy)]
    waits.append(columns(1, held_dpre) + fill(start, xs, held_x))
    last = []
    for which, (left, right) in enumerate(((held_hid, held_dy), (held_dpre, held_x))):
        for w in waits[which]:
            w.wait()
        for half in (1, 0):
            part = mm(left[pl.ds(half * units, units), :], right[...], NN).astype(BF)
            spot = pl.ds(which * units if half else 0, units)
            target = 2 if half else which
            stored[target][spot, :] = part
            last.append(start(stored[target].at[spot], outs[target].at[spot]))
    for c in last:
        c.wait()


def combine_kernel(experts, cap, names_ref, gates_ref, ret_ref, dx_ref, gate_ref):
    names = names_ref[...].astype(F32)
    pos = positions(names, experts)
    span = ret_ref.shape[0] // experts
    own, _, slot = row_owner(experts, span)
    picker = mm(own, pos.astype(BF), NN) == slot
    dx_ref[...] = mm(ones(picker), ret_ref[...], TN).astype(BF)
    table = mm(spare(experts, span, cap, True), ret_ref[:, 0:LANES], NN)
    table = table + mm(spare(experts, span, cap + 1, True), ret_ref[:, 0:LANES], NN)
    value = jnp.zeros(pos.shape, F32)
    for s in range(cap):
        value = jnp.where(pos == float(s), table[:, s : s + 1], value)
    expert = lax.broadcasted_iota(jnp.int32, pos.shape, 0).astype(F32)
    sums = [
        jnp.sum(jnp.where(expert == names[k : k + 1], value, 0.0), axis=0, keepdims=True)
        for k in range(2)
    ]
    line = lax.broadcasted_iota(jnp.int32, gate_ref.shape, 0)
    gate_ref[...] = jnp.where(line == 0, sums[0], sums[1]) / gates_ref[...]


def call(kernel, outs, vmem, **more):
    return pl.pallas_call(
        kernel,
        out_shape=outs,
        compiler_params=pltpu.CompilerParams(vmem_limit_bytes=vmem * MIB),
        cost_estimate=pl.CostEstimate(flops=1, bytes_accessed=1, transcendentals=0),
        **more,
    )


def shift(value, axis, by):
    size = lax.axis_size(axis)
    return lax.ppermute(value, axis, [(i, (i + by) % size) for i in range(size)])


def exchange(value):
    return lax.all_to_all(value, "expert", split_axis=0, concat_axis=0, tiled=True)


def local(hidden_in, grad_out, combine, routes, w_in, w_out):
    tokens, width = hidden_in.shape
    units = w_out.shape[1]
    experts = lax.axis_size("expert")
    planes = lax.axis_size("dp")
    names, gates = routes.T, combine.T
    wi, wo = w_in[0].T, w_out[0]
    hidden_units = 2 * units
    block = experts * CAP
    after = lax.optimization_barrier

    def arr(*shape, kind=BF):
        return jax.ShapeDtypeStruct(shape, kind)

    msg = call(message_kernel, arr(tokens + META, width), SMALL)(grad_out, names, gates)
    msgs = {0: msg}
    for k in (1, 3, 2):
        msgs[k] = shift(msg, "dp", k)
    xs = call(functools.partial(pick_kernel, experts), arr(experts * eights(CAP), width), LARGE)(
        hidden_in, names
    )
    wi, wo, _ = after((wi, wo, xs))
    wi_other, wo_other = shift(wi, "seq", 1), shift(wo, "seq", 1)
    msgs[1], wi_other, wo_other = after((msgs[1], wi_other, wo_other))
    xa, msgs[1], msgs[3] = after((exchange(xs), msgs[1], msgs[3]))
    x = call(functools.partial(split_kernel, experts), arr(block, width), SMALL)(xa)
    x, msgs[1] = after((x, msgs[1]))
    near = [shift(x, "dp", 1), shift(x, "dp", -1)]
    def expand(g):
        return call(
            functools.partial(expand_kernel, experts, CAP),
            arr(block * len(GROUPS[g]), width),
            SMALL,
        )(*(msgs[k] for k in GROUPS[g]))

    sent, msgs[2] = after((expand(0), msgs[2]))
    got = exchange(sent)
    sent, got, near = after((expand(1), got, near))
    got = [got, exchange(sent)]
    far, near = after((x, near))
    xs = {0: [x], 1: near[:1], 2: [shift(far, "dp", 2)], 3: near[1:]}

    def rows_call(g):
        blocks = len(GROUPS[g])
        count = blocks * block
        parts = sum((xs[k] for k in GROUPS[g]), [])
        hid, dpre, dy, *dx = call(
            functools.partial(rows_kernel, experts, len(parts), blocks),
            [arr(hidden_units, count)] * 2
            + [arr(count, width)]
            + [arr(block + META, width)] * blocks,
            LARGE,
            in_specs=[HBM] * (len(parts) + 5),
            out_specs=[HBM] * (3 + blocks),
            scratch_shapes=[pltpu.VMEM((count, width), BF)] * 3
            + [pltpu.VMEM((hidden_units, width), BF)] * 2
            + [pltpu.VMEM((hidden_units, count), BF)] * 2
            + [pltpu.VMEM((count + META * blocks, width), BF), pltpu.VMEM((META, count), BF)]
            + [pltpu.SemaphoreType.DMA((32,))],
        )(*parts, got[g], wi, wi_other, wo, wo_other)
        return [hid, dpre, dy], parts, dict(zip(GROUPS[g], dx))

    done_a, parts_a, dx = rows_call(0)
    dx = {k: shift(v, "dp", -k) for k, v in dx.items()}
    done_b, parts_b, dx_b = rows_call(1)
    dx[0], dx[2] = dx_b[0], shift(dx_b[2], "dp", 2)
    grads = [(units, width)] * 2 + [(2 * units, width)]
    total = planes * block
    ins = done_a + done_b + parts_a + parts_b
    mine_o, mine_i, theirs = call(
        functools.partial(weights_kernel, len(GROUPS), len(parts_a + parts_b)),
        [arr(*g) for g in grads],
        LARGE,
        in_specs=[HBM] * len(ins),
        out_specs=[HBM] * 3,
        scratch_shapes=[pltpu.VMEM((hidden_units, total), BF)] * 2
        + [pltpu.VMEM((total, width), BF)] * 2
        + [pltpu.VMEM(g, BF) for g in grads]
        + [pltpu.SemaphoreType.DMA((32,))],
    )(*ins)
    dx, theirs = after((dx, theirs))
    back = call(
        functools.partial(add_kernel, experts, CAP), arr(experts * eights(CAP), width), SMALL
    )(*(dx[k] for k in range(planes)))
    theirs, back = after((theirs, back))
    theirs = shift(theirs, "seq", 1).astype(F32)
    grad_wo = (mine_o.astype(F32) + theirs[:units]).astype(BF)
    grad_wi = (mine_i.astype(F32) + theirs[units:]).astype(BF)
    back, grad_wo, grad_wi = after((exchange(back), grad_wo, grad_wi))
    grad_x, grad_gate = call(
        functools.partial(combine_kernel, experts, CAP),
        [arr(tokens, width), arr(2, tokens, kind=F32)],
        SMALL,
    )(names, gates, back)
    return grad_x, grad_gate.T, grad_wi.T[None], grad_wo[None]


def solution(mesh):
    rows = P(("dp", "seq", "expert"), None)
    first = P("expert", None, ("dp", "seq"))
    second = P("expert", ("dp", "seq"), None)
    return jax.shard_map(
        local,
        mesh=mesh,
        in_specs=(rows, rows, rows, rows, first, second),
        out_specs=(rows, rows, first, second),
        check_vma=False,
    )
```
